32 devices in a mesh: groups: 2 (over y), ctx: 4 (over z), head: 4 (over x, core).
Axes of the slice: x: 2, y: 2, z: 4, core: 2. Of those that a mesh axis runs over, the one named last changes fastest.
Arguments:
- queries: bfloat16 [4096, 4096], P(('groups', 'ctx', 'head')), parts along dimension 0, may hold values from -6 to 6
- keys_in: bfloat16 [4096, 4096], P(('groups', 'ctx', 'head')), parts along dimension 0, may hold values from -6 to 6
- values: bfloat16 [4096, 4096], P(('groups', 'ctx', 'head')), parts along dimension 0, may hold values from -6 to 6
- doc_lengths: int32 [10], P('groups'), parts along dimension 0, may hold values from 1 to 512, 2048 in all
- rms_gain: float32 [4096], replicated, may hold values from 0.1 to 1.9
Outputs:
- mixed: bfloat16 [4096, 4096], P(('groups', 'ctx', 'head')), parts along dimension 0
The draws below stay inside these ranges and needn't reach their ends.
There are 2 independent parts, one for each index of `groups`. The reference program is written for one: setup_inputs(seed, part) draws one part's arguments, and reference() takes and returns one part's arrays. A program takes and returns all parts, laid end to end along the dimension named above; an argument that names none is the same for every part. Nothing has to cross between parts.
Inputs may be any that keep to these rules, and one draw needn't show every extreme that they name: `doc_lengths`: the lengths of the 5 documents sum to 2048, and the longest has exactly 512 tokens.
All inputs are finite; a program needn't handle non-finite values.
Results may differ from the reference program's by a relative error of at most 0.006.
Values may be sent and summed in bfloat16 or wider, within the bound.
No kernel may reach another device: no remote copies, remote signals or barrier semaphores. Data moves between devices by JAX's collectives and lax.ppermute only.
A program may use at most 64 MiB of HBM per device.

```python
import math
import jax
import jax.numpy as jnp
import numpy as np
from jax import lax

H = 32
DH = 128
SHARD = 512
TOKENS = 2048
MOST_DOC = 512
DOCS = 5
N_CTX = 4


def level_of(own_key, extent, cuts, low, largest):
    factor_of, own = 1.0, jax.random.fold_in(own_key, 6)
    for position, shards_of in cuts:
        heights = jnp.exp(jax.random.uniform(jax.random.fold_in(own, position), (shards_of,), jnp.float32, low / len(cuts), largest / len(cuts)))
        factor_of = factor_of * jnp.repeat(heights, extent[position] // shards_of).reshape([-1 if axis == position else 1 for axis in range(len(extent))])
    return factor_of


def length_profile(amount, total, most, skew):
    weights = [(1 << 20) // math.isqrt(rank ** skew) + 1 for rank in range(2, amount + 1)]
    spare, counts = total - most - (amount - 1), [1] * (amount - 1)
    while spare > 0:
        candidates = [i for i in range(amount - 1) if counts[i] < most]
        mass, left = sum([weights[i] for i in candidates]), spare
        for i in candidates:
            extra = min(most - counts[i], max(1, left * weights[i] // mass), spare)
            counts[i] = counts[i] + extra
            spare = spare - extra
    return np.array([most] + counts)


def ragged(key, number_of, total, reach, skew):
    if number_of == 2:
        one = jax.random.randint(key, (), max(1, total - reach), min(reach, total - 1) + 1)
        return jnp.stack([one, total - one])
    lengths = jnp.asarray(length_profile(number_of, total, reach, skew), jnp.int32)
    twos = (number_of - 1) // 2
    donor, taker = lengths[1:1 + 2 * twos:2], lengths[2:2 + 2 * twos:2]
    room = jnp.minimum(donor - 1, reach - taker)
    passed = jax.random.randint(jax.random.fold_in(key, 1), (twos,), 0, 1 << 20) % (room + 1)
    lengths = lengths.at[1:1 + 2 * twos:2].set(donor - passed).at[2:2 + 2 * twos:2].set(taker + passed)
    return lengths[jax.random.permutation(jax.random.fold_in(key, 2), number_of)]


def bell_draw(key, shape, spread, bound, split=(), kind=jnp.bfloat16):
    result = spread * jax.random.normal(key, shape, jnp.float32)
    if split:
        result = result * level_of(key, shape, split, -0.22, 0.18)
    return jnp.clip(result, -bound, bound).astype(kind)


def setup_inputs(seed: int = 0, part: int = 0) -> dict:
    keys = jax.random.split(jax.random.key(seed), 6)
    part_keys = jax.random.split(jax.random.fold_in(keys[5], part), 6)
    return {
        "queries": bell_draw(part_keys[0], (TOKENS, H * DH), 1.0, 6.0, ((0, 16),)),
        "keys_in": bell_draw(part_keys[1], (TOKENS, H * DH), 1.0, 6.0, ((0, 16),)),
        "values": bell_draw(part_keys[2], (TOKENS, H * DH), 1.0, 6.0, ((0, 16),)),
        "doc_lengths": ragged(part_keys[3], DOCS, TOKENS, MOST_DOC, 1).astype(jnp.int32),
        "rms_gain": jnp.clip(1.0 + 0.18 * jax.random.normal(keys[4], (H * DH,), jnp.float32), 0.1, 1.9),
    }


def doc_ids(doc_lengths, positions):
    doc_ends = jnp.cumsum(doc_lengths).astype(jnp.int32)
    counted = lax.optimization_barrier(jnp.sum((positions[:, None] >= doc_ends[None, :]).astype(jnp.int32), axis=1))
    return jnp.where(positions < 0, -1, counted).astype(jnp.int32)

def local_part(q_shard, k_shard, v_shard, segment):
    shard_rows = q_shard.shape[0]
    block_rows = min(512, shard_rows)
    order = jnp.arange(shard_rows, dtype=jnp.int32)
    pieces = []
    for block_id in range(shard_rows // block_rows):
        first_row = block_id * block_rows
        last_row = first_row + block_rows
        scores = jnp.einsum('qhd,khd->hqk', q_shard[first_row:last_row].astype(jnp.float32), k_shard[:last_row].astype(jnp.float32), precision=lax.Precision.HIGHEST)
        allowed = (segment[first_row:last_row, None] == segment[None, :last_row]) & (order[first_row:last_row, None] >= order[None, :last_row])
        weights = jnp.where(allowed[None], scores, 0.0).astype(jnp.bfloat16)
        weights = lax.optimization_barrier(weights)
        pieces.append(jnp.einsum('hqk,khd->qhd', weights.astype(jnp.float32), v_shard[:last_row].astype(jnp.float32), precision=lax.Precision.HIGHEST))
    return jnp.concatenate(pieces, axis=0)

def reference(queries, keys_in, values, doc_lengths, rms_gain):
    shape_four = (N_CTX, SHARD, H, DH)
    q_all = jax.nn.silu(queries.astype(jnp.float32)).astype(jnp.bfloat16).reshape(shape_four)
    k_all = jax.nn.silu(keys_in.astype(jnp.float32)).astype(jnp.bfloat16).reshape(shape_four)
    v_all = values.reshape(shape_four)

    def shard_step(carried, inputs):
        q_shard, k_shard, v_shard, shard_id = inputs
        shard_start = (shard_id * SHARD).astype(jnp.int32)
        positions = shard_start + jnp.arange(SHARD, dtype=jnp.int32)
        segment = doc_ids(doc_lengths, positions)
        before = doc_ids(doc_lengths, jnp.reshape(shard_start - 1, (1,)).astype(jnp.int32))[0]
        local = local_part(q_shard, k_shard, v_shard, segment)
        inter = jnp.einsum('shd,hde->she', q_shard.astype(jnp.float32), carried, precision=lax.Precision.HIGHEST)
        joined = (segment == before)[:, None, None]
        attended = (local + jnp.where(joined, inter, 0.0)).astype(jnp.bfloat16)
        keep = (segment == segment[-1])[:, None, None]
        masked_keys = jnp.where(keep, k_shard, jnp.zeros_like(k_shard))
        tail = jnp.einsum('shd,she->hde', masked_keys.astype(jnp.float32), v_shard.astype(jnp.float32), precision=lax.Precision.HIGHEST)
        carried = jnp.where(segment[-1] != before, tail, carried + tail)
        return (carried, attended)
    start_state = jnp.zeros((H, DH, DH), jnp.float32)
    final_state, attended = lax.scan(shard_step, start_state, (q_all, k_all, v_all, jnp.arange(N_CTX, dtype=jnp.int32)))
    output = attended.reshape(TOKENS, H * DH).astype(jnp.float32)
    meansq = lax.optimization_barrier(jnp.mean(output * output, axis=1, keepdims=True))
    return (output * lax.rsqrt(meansq + 1e-05) * rms_gain.astype(jnp.float32)).astype(jnp.bfloat16)
```

```python
import functools
import jax
import jax.numpy as jnp
from jax import lax
from jax.experimental import pallas as pl
from jax.experimental.pallas import tpu as pltpu
from jax.sharding import PartitionSpec as P

DH = 128
F32, BF16 = jnp.float32, jnp.bfloat16
VMEM_LIMIT = 32 << 20


def silu(x):
    x = x.astype(F32)
    return x / (1.0 + jnp.exp(-x))


def doc_start(len_ref, position):
    start = jnp.zeros_like(position)
    end = jnp.int32(0)
    for doc in range(len_ref.shape[0]):
        end = end + len_ref[doc]
        start = jnp.where(position >= end, end, start)
    return start


def same_doc(len_ref, earlier, later):
    return doc_start(len_ref, later) <= earlier


def state_kernel(rows, len_ref, at_ref, k_ref, v_ref, t_ref):
    first = at_ref[0] * rows
    kept = doc_start(len_ref, first + rows - 1) - first
    keep = lax.broadcasted_iota(jnp.int32, (rows, DH), 0) >= kept
    for h in range(t_ref.shape[0]):
        cols = slice(h * DH, (h + 1) * DH)
        k = jnp.where(keep, silu(k_ref[:, cols]), 0.0).astype(BF16)
        t = lax.dot_general(k, v_ref[:, cols], (((0,), (0,)), ((), ())), preferred_element_type=F32)
        t_ref[h] = t.astype(t_ref.dtype)


def states(lens, at, k, v, first_head, heads, heads_total, dtype):
    rows = k.shape[0]
    step = min(8, heads)
    spec = pl.BlockSpec((rows, step * DH), lambda i, n, a: (0, first_head(a) // step + i))
    return pl.pallas_call(
        functools.partial(state_kernel, rows),
        out_shape=jax.ShapeDtypeStruct((heads, DH, DH), dtype),
        grid_spec=pltpu.PrefetchScalarGridSpec(
            num_scalar_prefetch=2,
            grid=(heads // step,),
            in_specs=[spec, spec],
            out_specs=pl.BlockSpec((step, DH, DH), lambda i, n, a: (i, 0, 0)),
        ),
        compiler_params=pltpu.CompilerParams(vmem_limit_bytes=VMEM_LIMIT),
        cost_estimate=pl.CostEstimate(
            flops=2 * heads * rows * DH * DH, bytes_accessed=heads * DH * (4 * rows + 2 * DH), transcendentals=heads * rows * DH
        ),
    )(lens, at, k, v)


def chip_kernel(rows, len_ref, at_ref, own_ref, got_ref, p1_ref, a_ref, b_ref):
    at = at_ref[0]
    core, x = at % 2, (at // 2) % 2
    low = at - core
    whole = same_doc(len_ref, low * rows + rows - 1, (low + 2) * rows - 1)
    w_own = jnp.where((core == 1) | whole, 1.0, 0.0)
    w_got = jnp.where((core == 0) | whole, 1.0, 0.0)
    half = a_ref.shape[0]
    for h in range(2 * half):
        s = (own_ref[h].astype(F32) * w_own + got_ref[h].astype(F32) * w_got).astype(BF16)
        if h < half:
            a_ref[h] = s

            @pl.when(x == 0)
            def _():
                p1_ref[h] = s
        else:
            b_ref[h - half] = s

            @pl.when(x == 1)
            def _():
                p1_ref[h - half] = s


def relay_kernel(rows, len_ref, at_ref, r2_ref, b_ref, p3_ref):
    x = (at_ref[0] // 2) % 2

    @pl.when(x == 0)
    def _():
        p3_ref[...] = b_ref[...]

    @pl.when(x == 1)
    def _():
        p3_ref[...] = r2_ref[...]


def carry_kernel(rows, len_ref, at_ref, r1_ref, b_ref, p4_ref):
    at = at_ref[0]
    x = (at // 2) % 2
    chip = at // 2 * 2 * rows
    goes_on = same_doc(len_ref, chip + 2 * rows - 1, chip + 4 * rows - 1)
    w_b = jnp.where((x == 1) | goes_on, 1.0, 0.0)
    w_r = jnp.where(x == 0, 1.0, 0.0)
    for h in range(p4_ref.shape[0]):
        p4_ref[h] = (b_ref[h].astype(F32) * w_b + r1_ref[h].astype(F32) * w_r).astype(BF16)


def join_kernel(rows, len_ref, at_ref, r1_ref, r2_ref, r3_ref, r4_ref, own_ref, got_ref, mine_ref, send_ref):
    at = at_ref[0]
    core, x = at % 2, (at // 2) % 2
    low = at - core
    chip = low * rows
    w = jnp.where(same_doc(len_ref, chip - 2 * rows - 1, chip - 1), 1.0, 0.0)
    on = jnp.where(same_doc(len_ref, chip - 1, chip + rows - 1), 1.0, 0.0)
    w4 = jnp.where(x == 0, 1.0, w)
    half = r1_ref.shape[0]
    for h in range(2 * half):
        if h < half:
            near = jnp.where(x == 0, r3_ref[h].astype(F32), r1_ref[h].astype(F32))
            p = near + w * r2_ref[h].astype(F32)
        else:
            near = jnp.where(x == 0, 0.0, r3_ref[h - half].astype(F32))
            p = near + w4 * r4_ref[h - half].astype(F32)
        low_t = jnp.where(core == 0, own_ref[h].astype(F32), got_ref[h].astype(F32))
        upper = (low_t + on * p).astype(BF16)
        p = p.astype(BF16)
        mine_ref[h] = jnp.where(core == 0, p, upper)
        send_ref[h] = jnp.where(core == 0, upper, p)


def small_call(kernel, rows, lens, at, ins, outs):
    vmem = pl.BlockSpec(memory_space=pltpu.VMEM)
    smem = pl.BlockSpec(memory_space=pltpu.SMEM)
    many = len(outs) > 1
    shapes = [jax.ShapeDtypeStruct(s, BF16) for s in outs]
    return pl.pallas_call(
        functools.partial(kernel, rows),
        out_shape=shapes if many else shapes[0],
        in_specs=[smem, smem] + [vmem] * len(ins),
        out_specs=[vmem] * len(outs) if many else vmem,
        compiler_params=pltpu.CompilerParams(vmem_limit_bytes=VMEM_LIMIT),
        cost_estimate=pl.CostEstimate(flops=1 << 20, bytes_accessed=2 << 20, transcendentals=0),
    )(lens, at, *ins)


def local_kernel(rows, len_ref, at_ref, q_ref, k_ref, v_ref, loc_ref, qm_ref):
    first = at_ref[0] * rows
    i = first + lax.broadcasted_iota(jnp.int32, (rows, rows), 0)
    j = first + lax.broadcasted_iota(jnp.int32, (rows, rows), 1)
    start = doc_start(len_ref, i)
    allowed = (j <= i) & (j >= start)
    i_q = first + lax.broadcasted_iota(jnp.int32, (rows, DH), 0)
    joined = doc_start(len_ref, i_q) < first
    for h in range(q_ref.shape[1] // DH):
        cols = slice(h * DH, (h + 1) * DH)
        q = silu(q_ref[:, cols])
        k = silu(k_ref[:, cols]).astype(BF16)
        qm_ref[:, cols] = jnp.where(joined, q, 0.0).astype(BF16)
        s = lax.dot_general(q.astype(BF16), k, (((1,), (1,)), ((), ())), preferred_element_type=F32)
        s = jnp.where(allowed, s, 0.0).astype(BF16)
        loc_ref[:, cols] = jnp.dot(s, v_ref[:, cols], preferred_element_type=F32)


def local_part(lens, at, q, k, v):
    rows, width = q.shape
    step = min(8 * DH, width)
    spec = pl.BlockSpec((rows, step), lambda i, n, a: (0, i))
    return pl.pallas_call(
        functools.partial(local_kernel, rows),
        out_shape=[jax.ShapeDtypeStruct((rows, width), F32), jax.ShapeDtypeStruct((rows, width), BF16)],
        grid_spec=pltpu.PrefetchScalarGridSpec(
            num_scalar_prefetch=2,
            grid=(width // step,),
            in_specs=[spec] * 3,
            out_specs=[spec, spec],
        ),
        compiler_params=pltpu.CompilerParams(vmem_limit_bytes=VMEM_LIMIT),
        cost_estimate=pl.CostEstimate(flops=4 * rows * rows * width, bytes_accessed=12 * rows * width, transcendentals=2 * rows * width),
    )(lens, at, q, k, v)


def final_kernel(off_ref, loc_ref, qm_ref, mine_ref, other_ref, gain_ref, out_ref, att_ref):
    rows, width = out_ref.shape
    half = mine_ref.shape[0]
    total = jnp.zeros((rows, 1), F32)
    for part, p_ref in ((0, mine_ref), (1, other_ref)):
        base = jnp.where(off_ref[0] == part, 0, half * DH)
        for h in range(half):
            cols = pl.ds(pl.multiple_of(base + h * DH, DH), DH)
            att = loc_ref[:, cols] + jnp.dot(qm_ref[:, cols], p_ref[h], preferred_element_type=F32)
            att = att.astype(BF16)
            att_ref[:, cols] = att
            wide = att.astype(F32)
            total = total + jnp.sum(wide * wide, axis=1, keepdims=True)
    scale = lax.rsqrt(total / width + 1e-5)
    for h in range(2 * half):
        cols = slice(h * DH, (h + 1) * DH)
        out_ref[:, cols] = (att_ref[:, cols].astype(F32) * scale * gain_ref[:, cols]).astype(BF16)


def final(off, loc, qm, mine, other, gain):
    rows, width = loc.shape
    vmem = pl.BlockSpec(memory_space=pltpu.VMEM)
    return pl.pallas_call(
        final_kernel,
        out_shape=jax.ShapeDtypeStruct((rows, width), BF16),
        in_specs=[pl.BlockSpec(memory_space=pltpu.SMEM)] + [vmem] * 5,
        out_specs=vmem,
        scratch_shapes=[pltpu.VMEM((rows, width), BF16)],
        compiler_params=pltpu.CompilerParams(vmem_limit_bytes=VMEM_LIMIT),
        cost_estimate=pl.CostEstimate(flops=2 * rows * DH * width, bytes_accessed=12 * rows * width, transcendentals=rows),
    )(off, loc, qm, mine, other, gain.reshape(1, width))


def general(lens, at, q, k, v, gain):
    rows, width = q.shape
    heads = width // DH
    blocks = lax.axis_size("ctx") * lax.axis_size("head")
    axes = ("ctx", "head")
    state = states(lens, at, k, v, lambda a: 0, heads, heads, F32)
    me = at[0]
    ends = jnp.cumsum(lens)

    def segment(position):
        return jnp.where(position < 0, -1, jnp.sum((position >= ends).astype(jnp.int32)))

    hop = 1
    while hop < blocks:
        came = lax.ppermute(state, axes, [(b, b + hop) for b in range(blocks - hop)])
        adds = segment((me + 1) * rows - 1) == segment((me + 1 - hop) * rows - 1)
        state = state + jnp.where(adds, came, 0.0)
        hop *= 2
    before = lax.ppermute(state, axes, [(b, b + 1) for b in range(blocks - 1)]).astype(BF16)
    loc, qm = local_part(lens, at, q, k, v)
    return final(jnp.zeros((1,), jnp.int32), loc, qm, before[: heads // 2], before[heads // 2 :], gain)


def neighbours(lens, at, q, k, v, gain):
    rows, width = q.shape
    heads = width // DH
    half, chunk = heads // 2, heads // 4
    ctx_parts = lax.axis_size("ctx")
    pair = [(0, 1), (1, 0), (2, 3), (3, 2)]
    across = [(0, 2), (2, 0), (1, 3), (3, 1)]
    onward = [(c, (c + 1) % ctx_parts) for c in range(ctx_parts)]
    theirs = states(lens, at, k, v, lambda a: (1 - a[0] % 2) * half, half, heads, BF16)
    got = lax.ppermute(theirs, "head", pair)
    own = states(lens, at, k, v, lambda a: a[0] % 2 * half, half, heads, BF16)
    part = (chunk, DH, DH)
    p1, a, b = small_call(chip_kernel, rows, lens, at, [own, got], [part] * 3)
    r1 = lax.ppermute(p1, "head", across)
    r2 = lax.ppermute(a, "ctx", onward)
    loc, qm = local_part(lens, at, q, k, v)
    p4 = small_call(carry_kernel, rows, lens, at, [r1, b], [part])
    r4 = lax.ppermute(p4, "ctx", onward)
    p3 = small_call(relay_kernel, rows, lens, at, [r2, b], [part])
    r3 = lax.ppermute(p3, "head", across)
    mine, send = small_call(join_kernel, rows, lens, at, [r1, r2, r3, r4, own, got], [(half, DH, DH)] * 2)
    other = lax.ppermute(send, "head", pair)
    return final(at % 2, loc, qm, mine, other, gain)


def per_device(queries, keys_in, values, doc_lengths, rms_gain):
    head_parts = lax.axis_size("head")
    at = jnp.reshape(lax.axis_index(("ctx", "head")).astype(jnp.int32), (1,))
    args = (doc_lengths, at, queries, keys_in, values, rms_gain)
    if head_parts != 4:
        return general(*args)
    shard_rows = queries.shape[0] * head_parts
    return lax.cond(jnp.max(doc_lengths) <= shard_rows, neighbours, general, *args)


def solution(mesh):
    return jax.shard_map(
        per_device,
        mesh=mesh,
        in_specs=(
            P(("groups", "ctx", "head"), None),
            P(("groups", "ctx", "head"), None),
            P(("groups", "ctx", "head"), None),
            P("groups"),
            P(),
        ),
        out_specs=P(("groups", "ctx", "head"), None),
        check_vma=False,
    )
```

```python
import functools
import jax
import jax.numpy as jnp
from jax import lax
from jax.experimental import pallas as pl
from jax.experimental.pallas import tpu as pltpu
from jax.sharding import PartitionSpec as P

DH = 128
F32, BF16 = jnp.float32, jnp.bfloat16
VMEM = pl.BlockSpec(memory_space=pltpu.VMEM)
SMEM = pl.BlockSpec(memory_space=pltpu.SMEM)
HBM = pl.BlockSpec(memory_space=pltpu.HBM)
PARAMS = pltpu.CompilerParams(vmem_limit_bytes=12 << 20)
W_OWN, W_GOT, W_NEXT, W_FAR, W_ON, IS_X1, IS_CORE1 = range(7)


def silu(x):
    half = x.astype(F32) * 0.5
    return half + half * jnp.tanh(half)


def doc_start(len_ref, position):
    start = jnp.zeros_like(position)
    end = jnp.int32(0)
    for doc in range(len_ref.shape[0]):
        end = end + len_ref[doc]
        start = jnp.where(position >= end, end, start)
    return start


def same_doc(len_ref, earlier, later):
    return doc_start(len_ref, later) <= earlier


def columns(start, heads):
    return pl.ds(pl.multiple_of(start, DH), heads * DH)


def cost(flops, nbytes, trans=0):
    return pl.CostEstimate(flops=flops, bytes_accessed=nbytes, transcendentals=trans)


def block_states(len_ref, at, k_ref, v_ref, t_ref, base, heads, ready=None):
    rows = k_ref.shape[0]
    first = at * rows
    keep = lax.broadcasted_iota(jnp.int32, (rows, DH), 0) >= doc_start(len_ref, first + rows - 1) - first
    for h in range(heads):
        if ready is not None:
            ready(h)
        cols = columns(base + h * DH, 1)
        k = jnp.where(keep, silu(k_ref[:, cols]), 0.0).astype(BF16)
        t = lax.dot_general(k, v_ref[:, cols], (((0,), (0,)), ((), ())), preferred_element_type=F32)
        t_ref[h] = t.astype(t_ref.dtype)


def state_kernel(offset, len_ref, at_ref, k_ref, v_ref, t_ref):
    at = at_ref[0]
    block_states(len_ref, at, k_ref, v_ref, t_ref, offset(at), t_ref.shape[0])


def opening_kernel(pieces, len_ref, at_ref, k_hbm, v_hbm, t_ref, w_ref, k_ref, v_ref, sems):
    at = at_ref[0]
    core, x = at % 2, (at // 2) % 2
    half, rows = t_ref.shape[0], k_ref.shape[0]
    theirs, mine = (1 - core) * half * DH, core * half * DH
    step = half // pieces
    copies = []
    for piece in range(pieces + 1):
        cols = columns(theirs + piece * step * DH, step) if piece < pieces else columns(mine, half)
        pairs = ((k_hbm, k_ref), (v_hbm, v_ref))
        copies.append([pltpu.make_async_copy(src.at[:, cols], dst.at[:, cols], sems.at[piece, n]) for n, (src, dst) in enumerate(pairs)])
        for copy in copies[-1]:
            copy.start()
    chip = (at - core) * rows
    whole = same_doc(len_ref, chip + rows - 1, chip + 2 * rows - 1)
    values = {
        W_OWN: (core == 1) | whole,
        W_GOT: (core == 0) | whole,
        W_NEXT: same_doc(len_ref, chip + 2 * rows - 1, chip + 4 * rows - 1),
        W_FAR: same_doc(len_ref, chip - 2 * rows - 1, chip - 1),
        W_ON: same_doc(len_ref, chip - 1, chip + rows - 1),
        IS_X1: x == 1,
        IS_CORE1: core == 1,
    }
    for row, value in values.items():
        w_ref[row : row + 1, :] = jnp.full((1, DH), jnp.where(value, 1.0, 0.0), F32)

    def ready(h):
        if h % step == 0:
            for copy in copies[h // step]:
                copy.wait()

    block_states(len_ref, at, k_ref, v_ref, t_ref, theirs, half, ready)
    for copy in copies[pieces]:
        copy.wait()


def opening(lens, at, k, v, half):
    pieces = 4 if half % 4 == 0 else 1
    rows = k.shape[0]
    vmem = jax.ShapeDtypeStruct(k.shape, BF16)
    return pl.pallas_call(
        functools.partial(opening_kernel, pieces),
        out_shape=[jax.ShapeDtypeStruct((half, DH, DH), BF16), jax.ShapeDtypeStruct((8, DH), F32), vmem, vmem],
        in_specs=[SMEM, SMEM, HBM, HBM],
        out_specs=[VMEM] * 4,
        scratch_shapes=[pltpu.SemaphoreType.DMA((pieces + 1, 2))],
        compiler_params=PARAMS,
        cost_estimate=cost(2 * half * rows * DH * DH, 4 * k.size, half * rows * DH),
    )(lens, at, k, v)


def states(lens, at, k, v, offset, heads, dtype):
    rows = k.shape[0]
    return pl.pallas_call(
        functools.partial(state_kernel, offset),
        out_shape=jax.ShapeDtypeStruct((heads, DH, DH), dtype),
        in_specs=[SMEM, SMEM, VMEM, VMEM],
        out_specs=VMEM,
        compiler_params=PARAMS,
        cost_estimate=cost(2 * heads * rows * DH * DH, heads * DH * (4 * rows + 2 * DH), heads * rows * DH),
    )(lens, at, k, v)


def weight(w_ref, row):
    return jnp.broadcast_to(w_ref[row : row + 1, :], (DH, DH)).astype(BF16)


def chip_kernel(w_ref, own_ref, got_ref, a_ref, b_ref):
    w_own, w_got = weight(w_ref, W_OWN), weight(w_ref, W_GOT)
    cut = a_ref.shape[0]
    for h in range(own_ref.shape[0]):
        s = own_ref[h] * w_own + got_ref[h] * w_got
        if h < cut:
            a_ref[h] = s
        else:
            b_ref[h - cut] = s


def relay_kernel(w_ref, a_ref, r2_ref, p3_ref):
    is_x1 = weight(w_ref, IS_X1)
    is_x0 = 1.0 - is_x1
    for h in range(p3_ref.shape[0]):
        p3_ref[h] = r2_ref[h] * is_x1 + a_ref[h] * is_x0


def carry_kernel(w_ref, b_ref, r1_ref, p4_ref):
    is_x1, w_next = weight(w_ref, IS_X1), weight(w_ref, W_NEXT)
    w_r = 1.0 - is_x1
    w_b = is_x1 + w_r * w_next
    for h in range(p4_ref.shape[0]):
        p4_ref[h] = b_ref[h] * w_b + r1_ref[h] * w_r


def join_kernel(start, first_row, near_ref, far_ref, w_ref, own_ref, got_ref, mine_ref, send_ref):
    w, on, is_x1, core1 = (weight(w_ref, row) for row in (W_FAR, W_ON, IS_X1, IS_CORE1))
    core0 = 1.0 - core1
    if first_row:
        w_near = None
    else:
        w_near = is_x1
        w = is_x1 * w + (1.0 - is_x1)
    m1, m2 = core1 * on + core0, core0 * on + core1
    for h in range(mine_ref.shape[0]):
        near = near_ref[h] if w_near is None else near_ref[h] * w_near
        p = near + far_ref[h] * w
        mine_ref[h] = p * m1 + got_ref[start + h] * core1
        send_ref[h] = p * m2 + own_ref[start + h] * core0


def small_call(kernel, ins, outs):
    many = len(outs) > 1
    shapes = [jax.ShapeDtypeStruct(s, BF16) for s in outs]
    return pl.pallas_call(
        kernel,
        out_shape=shapes if many else shapes[0],
        in_specs=[VMEM] * len(ins),
        out_specs=[VMEM] * len(outs) if many else VMEM,
        compiler_params=PARAMS,
        cost_estimate=cost(1 << 20, 1 << 20),
    )(*ins)


def local_kernel(offset, len_ref, at_ref, q_ref, k_ref, v_ref, loc_ref, qm_ref):
    rows = q_ref.shape[0]
    at = at_ref[0]
    first = at * rows
    i = first + lax.broadcasted_iota(jnp.int32, (rows, rows), 0)
    j = first + lax.broadcasted_iota(jnp.int32, (rows, rows), 1)
    start = doc_start(len_ref, i)
    allowed = (j <= i) & (j >= start)
    i_q = first + lax.broadcasted_iota(jnp.int32, (rows, DH), 0)
    joined = doc_start(len_ref, i_q) < first
    base = offset(at)
    for h in range(loc_ref.shape[1] // DH):
        cols, here = columns(base + h * DH, 1), slice(h * DH, (h + 1) * DH)
        q = silu(q_ref[:, cols])
        k = silu(k_ref[:, cols]).astype(BF16)
        qm_ref[:, here] = jnp.where(joined, q, 0.0).astype(BF16)
        s = lax.dot_general(q.astype(BF16), k, (((1,), (1,)), ((), ())), preferred_element_type=F32)
        s = jnp.where(allowed, s, 0.0).astype(BF16)
        loc_ref[:, here] = jnp.dot(s, v_ref[:, cols], preferred_element_type=F32)


def local_part(lens, at, q, k, v, offset, heads):
    rows = q.shape[0]
    width = heads * DH
    return pl.pallas_call(
        functools.partial(local_kernel, offset),
        out_shape=[jax.ShapeDtypeStruct((rows, width), F32), jax.ShapeDtypeStruct((rows, width), BF16)],
        in_specs=[SMEM, SMEM, VMEM, VMEM, VMEM],
        out_specs=[VMEM, VMEM],
        compiler_params=PARAMS,
        cost_estimate=cost(4 * rows * rows * width, 12 * rows * width, 2 * rows * width),
    )(lens, at, q, k, v)


def attend(loc_ref, qm_ref, p_refs, att_ref):
    total = jnp.zeros((att_ref.shape[0], DH), F32)
    h = 0
    for p_ref in p_refs:
        for n in range(p_ref.shape[0]):
            cols = slice(h * DH, (h + 1) * DH)
            att = loc_ref[:, cols] + jnp.dot(qm_ref[:, cols], p_ref[n], preferred_element_type=F32)
            att = att.astype(BF16)
            att_ref[:, cols] = att
            wide = att.astype(F32)
            total = total + wide * wide
            h += 1
    return total


def attend_any(far_ref, scanned_ref, start, loc_ref, qm_ref, p_refs, att_ref, sum_ref, scan_ref, sem):
    @pl.when(far_ref[0] == 0)
    def _():
        sum_ref[...] = attend(loc_ref, qm_ref, p_refs, att_ref)

    @pl.when(far_ref[0] != 0)
    def _():
        copy = pltpu.make_async_copy(scanned_ref.at[pl.ds(start, scan_ref.shape[0])], scan_ref, sem)
        copy.start()
        copy.wait()
        sum_ref[...] = attend(loc_ref, qm_ref, [scan_ref], att_ref)


def first_kernel(at_ref, far_ref, loc_ref, qm_ref, pa_ref, pb_ref, scanned_ref, att_ref, sum_ref, scan_ref, sem):
    start = at_ref[0] % 2 * scan_ref.shape[0]
    attend_any(far_ref, scanned_ref, start, loc_ref, qm_ref, [pa_ref, pb_ref], att_ref, sum_ref, scan_ref, sem)


def last_kernel(
    pieces, at_ref, far_ref, loc_ref, qm_ref, pa_ref, pb_ref, scanned_ref, att0_ref, sum0_ref, gain_ref,
    out_ref, att_ref, sum_ref, done_ref, scan_ref, sem, sems,
):
    half = scan_ref.shape[0]
    core = at_ref[0] % 2
    attend_any(far_ref, scanned_ref, (1 - core) * half, loc_ref, qm_ref, [pa_ref, pb_ref], att_ref, sum_ref, scan_ref, sem)
    width = 2 * half * DH
    total = jnp.sum(sum_ref[...] + sum0_ref[...], axis=1, keepdims=True)
    scale = lax.rsqrt(total / width + 1e-5)
    step = half // pieces
    copies = []
    for part, src in enumerate((att0_ref, att_ref)):
        base = jnp.where(core == part, 0, half * DH)
        for piece in range(pieces):
            for h in range(piece * step, (piece + 1) * step):
                cols = slice(h * DH, (h + 1) * DH)
                gain = gain_ref[:, columns(base + h * DH, 1)]
                done_ref[part, :, cols] = (src[:, cols].astype(F32) * scale * gain).astype(BF16)
            cols = slice(piece * step * DH, (piece + 1) * step * DH)
            there = columns(base + piece * step * DH, step)
            copies.append(pltpu.make_async_copy(done_ref.at[part, :, cols], out_ref.at[:, there], sems.at[part, piece]))
            copies[-1].start()
    for copy in copies:
        copy.wait()


def empty_kernel(out_ref):
    pass


def scan(lens, at, k, v):
    rows, width = k.shape
    blocks = lax.axis_size("ctx") * lax.axis_size("head")
    axes = ("ctx", "head")
    state = states(lens, at, k, v, lambda a: 0, width // DH, F32)
    me = at[0]
    ends = jnp.cumsum(lens)

    def segment(position):
        return jnp.where(position < 0, -1, jnp.sum((position >= ends).astype(jnp.int32)))

    hop = 1
    while hop < blocks:
        came = lax.ppermute(state, axes, [(b, b + hop) for b in range(blocks - hop)])
        adds = segment((me + 1) * rows - 1) == segment((me + 1 - hop) * rows - 1)
        state = state + jnp.where(adds, came, 0.0)
        hop *= 2
    return lax.ppermute(state, axes, [(b, b + 1) for b in range(blocks - 1)]).astype(BF16)


def finish_first(at, far, loc, qm, pa, pb, scanned):
    rows, width = loc.shape
    return pl.pallas_call(
        first_kernel,
        out_shape=[jax.ShapeDtypeStruct((rows, width), BF16), jax.ShapeDtypeStruct((rows, DH), F32)],
        in_specs=[SMEM, SMEM] + [VMEM] * 4 + [HBM],
        out_specs=[VMEM, VMEM],
        scratch_shapes=[pltpu.VMEM((width // DH, DH, DH), BF16), pltpu.SemaphoreType.DMA],
        compiler_params=PARAMS,
        cost_estimate=cost(2 * rows * DH * width, 10 * rows * width),
    )(at, far, loc, qm, pa, pb, scanned)


def finish_last(at, far, loc, qm, pa, pb, scanned, att, total, gain):
    rows, half_width = loc.shape
    half = half_width // DH
    pieces = 2 if half % 2 == 0 else 1
    return pl.pallas_call(
        functools.partial(last_kernel, pieces),
        out_shape=jax.ShapeDtypeStruct((rows, 2 * half_width), BF16),
        in_specs=[SMEM, SMEM] + [VMEM] * 4 + [HBM] + [VMEM] * 3,
        out_specs=HBM,
        scratch_shapes=[
            pltpu.VMEM((rows, half_width), BF16),
            pltpu.VMEM((rows, DH), F32),
            pltpu.VMEM((2, rows, half_width), BF16),
            pltpu.VMEM((half, DH, DH), BF16),
            pltpu.SemaphoreType.DMA,
            pltpu.SemaphoreType.DMA((2, pieces)),
        ],
        compiler_params=PARAMS,
        cost_estimate=cost(2 * rows * DH * half_width, 12 * rows * half_width),
    )(at, far, loc, qm, pa, pb, scanned, att, total, gain.reshape(1, 2 * half_width))


def general(lens, at, q, k, v, gain):
    half = q.shape[1] // (2 * DH)
    cut = half // 2
    far = jnp.ones((1,), jnp.int32)
    even = at * 2
    scanned = scan(lens, at, k, v)
    loc0, qm0 = local_part(lens, at, q, k, v, lambda a: 0, half)
    loc1, qm1 = local_part(lens, at, q, k, v, lambda a: half * DH, half)
    att, total = finish_first(even, far, loc0, qm0, scanned[:cut], scanned[cut:half], scanned)
    return finish_last(even, far, loc1, qm1, scanned[half : half + cut], scanned[half + cut :], scanned, att, total, gain)


def neighbours(lens, at, q, k, v, gain):
    rows, width = q.shape
    heads = width // DH
    half = heads // 2
    cut = half // 2
    ctx_parts, head_parts = lax.axis_size("ctx"), lax.axis_size("head")
    pair = [(0, 1), (1, 0), (2, 3), (3, 2)]
    across = [(0, 2), (2, 0), (1, 3), (3, 1)]
    onward = [(c, (c + 1) % ctx_parts) for c in range(ctx_parts)]
    chunk_a, chunk_b = (cut, DH, DH), (half - cut, DH, DH)

    def own_half(a):
        return a % 2 * half * DH

    def other_half(a):
        return (1 - a % 2) * half * DH

    theirs, w, k_in, v_in = opening(lens, at, k, v, half)
    got = lax.ppermute(theirs, "head", pair)
    own = states(lens, at, k_in, v_in, own_half, half, BF16)
    a, b = small_call(chip_kernel, [w, own, got], [chunk_a, chunk_b])
    r2 = lax.ppermute(a, "ctx", onward)
    r1 = lax.ppermute(b, "head", across)
    loc0, qm0 = local_part(lens, at, q, k_in, v_in, own_half, half)
    far = (jnp.max(lens) > rows * head_parts).astype(jnp.int32)
    scanned = lax.cond(
        far > 0,
        lambda: scan(lens, at, k, v),
        lambda: pl.pallas_call(empty_kernel, out_shape=jax.ShapeDtypeStruct((heads, DH, DH), BF16), out_specs=HBM)(),
    )
    far = far.reshape(1)
    r2, loc0, scanned = lax.optimization_barrier((r2, loc0, scanned))
    p3 = small_call(relay_kernel, [w, a, r2], [chunk_a])
    r3 = lax.ppermute(p3, "head", across)
    p4 = small_call(carry_kernel, [w, b, r1], [chunk_b])
    r4 = lax.ppermute(p4, "ctx", onward)
    loc1, qm1 = local_part(lens, at, q, k_in, v_in, other_half, half)
    r3, loc1 = lax.optimization_barrier((r3, loc1))
    mine_a, send_a = small_call(functools.partial(join_kernel, 0, True), [r3, r2, w, own, got], [chunk_a] * 2)
    other_a = lax.ppermute(send_a, "head", pair)
    mine_b, send_b = small_call(functools.partial(join_kernel, cut, False), [r1, r4, w, own, got], [chunk_b] * 2)
    other_b = lax.ppermute(send_b, "head", pair)
    att, total = finish_first(at, far, loc0, qm0, mine_a, mine_b, scanned)
    return finish_last(at, far, loc1, qm1, other_a, other_b, scanned, att, total, gain)


def per_device(queries, keys_in, values, doc_lengths, rms_gain):
    at = jnp.reshape(lax.axis_index(("ctx", "head")).astype(jnp.int32), (1,))
    plan = neighbours if lax.axis_size("head") == 4 else general
    return plan(doc_lengths, at, queries, keys_in, values, rms_gain)


def solution(mesh):
    return jax.shard_map(
        per_device,
        mesh=mesh,
        in_specs=(
            P(("groups", "ctx", "head"), None),
            P(("groups", "ctx", "head"), None),
            P(("groups", "ctx", "head"), None),
            P("groups"),
            P(),
        ),
        out_specs=P(("groups", "ctx", "head"), None),
        check_vma=False,
    )
```

```python
import functools
import jax
import jax.numpy as jnp
from jax import lax
from jax.experimental import pallas as pl
from jax.experimental.pallas import tpu as pltpu
from jax.sharding import PartitionSpec as P

DH = 128
F32, BF16 = jnp.float32, jnp.bfloat16
VMEM = pl.BlockSpec(memory_space=pltpu.VMEM)
SMEM = pl.BlockSpec(memory_space=pltpu.SMEM)
HBM = pl.BlockSpec(memory_space=pltpu.HBM)
PARAMS = pltpu.CompilerParams(vmem_limit_bytes=12 << 20)
W_OWN, W_GOT, W_NEXT, W_FAR, W_ON, IS_X1, IS_CORE1 = range(7)
KEEP, ALLOWED, JOINED = range(3)
GROUP = 4


def in_hbm(x):
    return pltpu.with_memory_space_constraint(x, pltpu.HBM)


def silu(x):
    half = x.astype(F32) * 0.5
    return half + half * jnp.tanh(half)


def doc_start(len_ref, position):
    start = jnp.zeros_like(position)
    end = jnp.int32(0)
    for doc in range(len_ref.shape[0]):
        end = end + len_ref[doc]
        start = jnp.where(position >= end, end, start)
    return start


def same_doc(len_ref, earlier, later):
    return doc_start(len_ref, later) <= earlier


def columns(start, heads):
    return pl.ds(pl.multiple_of(start, DH), heads * DH)


def cost(flops, nbytes, trans=0):
    return pl.CostEstimate(flops=flops, bytes_accessed=nbytes, transcendentals=trans)


def make_masks(len_ref, at, rows):
    first = at * rows
    i = lax.broadcasted_iota(jnp.int32, (rows, DH), 0)
    keep = i >= doc_start(len_ref, first + rows - 1) - first
    start = doc_start(len_ref, first + i)
    joined = start < first
    i = lax.broadcasted_iota(jnp.int32, (rows, rows), 0)
    j = lax.broadcasted_iota(jnp.int32, (rows, rows), 1)
    allowed = (j <= i) & (j >= doc_start(len_ref, first + i) - first)
    return [jnp.where(mask, 1.0, 0.0).astype(BF16) for mask in (keep, allowed, joined)]


def block_states(keep, k_ref, v_ref, t_ref, base, heads, ready=None):
    for h0 in range(0, heads, GROUP):
        group = range(h0, min(h0 + GROUP, heads))
        sums = []
        for h in group:
            if ready is not None:
                ready(h)
            cols = columns(base + h * DH, 1)
            k = silu(k_ref[:, cols]).astype(BF16) * keep
            sums.append(lax.dot_general(k, v_ref[:, cols], (((0,), (0,)), ((), ())), preferred_element_type=F32))
        for h, t in zip(group, sums):
            t_ref[h] = t.astype(t_ref.dtype)


def own_kernel(offset, at_ref, m_ref, k_ref, v_ref, t_ref):
    block_states(m_ref[KEEP], k_ref, v_ref, t_ref, offset(at_ref[0]), t_ref.shape[0])


def opening_kernel(pieces, len_hbm, at_ref, k_hbm, v_hbm, t_ref, w_ref, m_ref, k_ref, v_ref, len_ref, sems, len_sem):
    at = at_ref[0]
    core, x = at % 2, (at // 2) % 2
    half, rows = t_ref.shape[0], k_ref.shape[0]
    len_copy = pltpu.make_async_copy(len_hbm, len_ref, len_sem)
    len_copy.start()
    theirs, mine = (1 - core) * half * DH, core * half * DH
    step = half // pieces
    copies = []
    for piece in range(pieces + 1):
        cols = columns(theirs + piece * step * DH, step) if piece < pieces else columns(mine, half)
        pairs = ((k_hbm, k_ref), (v_hbm, v_ref))
        copies.append([pltpu.make_async_copy(src.at[:, cols], dst.at[:, cols], sems.at[piece, n]) for n, (src, dst) in enumerate(pairs)])
        for copy in copies[-1]:
            copy.start()
    len_copy.wait()
    chip = (at - core) * rows
    whole = same_doc(len_ref, chip + rows - 1, chip + 2 * rows - 1)
    values = {
        W_OWN: (core == 1) | whole,
        W_GOT: (core == 0) | whole,
        W_NEXT: same_doc(len_ref, chip + 2 * rows - 1, chip + 4 * rows - 1),
        W_FAR: same_doc(len_ref, chip - 2 * rows - 1, chip - 1),
        W_ON: same_doc(len_ref, chip - 1, chip + rows - 1),
        IS_X1: x == 1,
        IS_CORE1: core == 1,
    }
    for row, value in values.items():
        w_ref[row : row + 1, :] = jnp.full((1, DH), jnp.where(value, 1.0, 0.0), F32)

    masks = make_masks(len_ref, at, rows)
    for n, mask in enumerate(masks):
        m_ref[n] = mask

    def ready(h):
        if h % step == 0:
            for copy in copies[h // step]:
                copy.wait()

    block_states(masks[KEEP], k_ref, v_ref, t_ref, theirs, half, ready)
    for copy in copies[pieces]:
        copy.wait()


def masks_kernel(rows, len_ref, at_ref, m_ref):
    for n, mask in enumerate(make_masks(len_ref, at_ref[0], rows)):
        m_ref[n] = mask


def masks_only(lens, at, rows):
    return pl.pallas_call(
        functools.partial(masks_kernel, rows),
        out_shape=jax.ShapeDtypeStruct((3, rows, DH), BF16),
        in_specs=[SMEM, SMEM],
        out_specs=VMEM,
        compiler_params=PARAMS,
        cost_estimate=cost(1 << 20, 6 * rows * DH),
    )(lens, at)


def opening(lens, at, k, v, half):
    pieces = 4 if half % 4 == 0 else 1
    rows = k.shape[0]
    vmem = jax.ShapeDtypeStruct(k.shape, BF16)
    return pl.pallas_call(
        functools.partial(opening_kernel, pieces),
        out_shape=[
            jax.ShapeDtypeStruct((half, DH, DH), BF16),
            jax.ShapeDtypeStruct((8, DH), F32),
            jax.ShapeDtypeStruct((3, rows, DH), BF16),
            vmem,
            vmem,
        ],
        in_specs=[HBM, SMEM, HBM, HBM],
        out_specs=[VMEM] * 5,
        scratch_shapes=[pltpu.SMEM(lens.shape, jnp.int32), pltpu.SemaphoreType.DMA((pieces + 1, 2)), pltpu.SemaphoreType.DMA],
        compiler_params=PARAMS,
        cost_estimate=cost(2 * half * rows * DH * DH, 4 * k.size, half * rows * DH),
    )(in_hbm(lens), at, in_hbm(k), in_hbm(v))


def states(at, masks, k, v, offset, heads, dtype):
    rows = k.shape[0]
    return pl.pallas_call(
        functools.partial(own_kernel, offset),
        out_shape=jax.ShapeDtypeStruct((heads, DH, DH), dtype),
        in_specs=[SMEM, VMEM, VMEM, VMEM],
        out_specs=VMEM,
        compiler_params=PARAMS,
        cost_estimate=cost(2 * heads * rows * DH * DH, heads * DH * (4 * rows + 2 * DH), heads * rows * DH),
    )(at, masks, k, v)


def weight(w_ref, row):
    return jnp.broadcast_to(w_ref[row : row + 1, :], (DH, DH)).astype(BF16)


def chip_kernel(w_ref, own_ref, got_ref, a_ref, b_ref):
    w_own, w_got = weight(w_ref, W_OWN), weight(w_ref, W_GOT)
    cut = a_ref.shape[0]
    for h in range(own_ref.shape[0]):
        s = own_ref[h] * w_own + got_ref[h] * w_got
        if h < cut:
            a_ref[h] = s
        else:
            b_ref[h - cut] = s


def relay_kernel(w_ref, a_ref, r2_ref, p3_ref):
    is_x1 = weight(w_ref, IS_X1)
    is_x0 = 1.0 - is_x1
    for h in range(p3_ref.shape[0]):
        p3_ref[h] = r2_ref[h] * is_x1 + a_ref[h] * is_x0


def carry_kernel(w_ref, b_ref, r1_ref, p4_ref):
    is_x1, w_next = weight(w_ref, IS_X1), weight(w_ref, W_NEXT)
    w_r = 1.0 - is_x1
    w_b = is_x1 + w_r * w_next
    for h in range(p4_ref.shape[0]):
        p4_ref[h] = b_ref[h] * w_b + r1_ref[h] * w_r


def join_kernel(start, first_row, near_ref, far_ref, w_ref, own_ref, got_ref, mine_ref, send_ref):
    w, on, is_x1, core1 = (weight(w_ref, row) for row in (W_FAR, W_ON, IS_X1, IS_CORE1))
    core0 = 1.0 - core1
    if first_row:
        w_near = None
    else:
        w_near = is_x1
        w = is_x1 * w + (1.0 - is_x1)
    m1, m2 = core1 * on + core0, core0 * on + core1
    for h in range(mine_ref.shape[0]):
        near = near_ref[h] if w_near is None else near_ref[h] * w_near
        p = near + far_ref[h] * w
        mine_ref[h] = p * m1 + got_ref[start + h] * core1
        send_ref[h] = p * m2 + own_ref[start + h] * core0


def small_call(kernel, ins, outs):
    many = len(outs) > 1
    shapes = [jax.ShapeDtypeStruct(s, BF16) for s in outs]
    return pl.pallas_call(
        kernel,
        out_shape=shapes if many else shapes[0],
        in_specs=[VMEM] * len(ins),
        out_specs=[VMEM] * len(outs) if many else VMEM,
        compiler_params=PARAMS,
        cost_estimate=cost(1 << 20, 1 << 20),
    )(*ins)


def local_kernel(offset, pieces, at_ref, m_ref, q_hbm, k_ref, v_ref, loc_ref, qm_ref, q_ref, sems):
    heads = loc_ref.shape[1] // DH
    base = offset(at_ref[0])
    step = heads // pieces
    copies = []
    for piece in range(pieces):
        here = slice(piece * step * DH, (piece + 1) * step * DH)
        copies.append(pltpu.make_async_copy(q_hbm.at[:, columns(base + piece * step * DH, step)], q_ref.at[:, here], sems.at[piece]))
        copies[-1].start()
    allowed, joined = m_ref[ALLOWED], m_ref[JOINED]
    for piece in range(pieces):
        copies[piece].wait()
        for h0 in range(piece * step, (piece + 1) * step, GROUP):
            group = range(h0, min(h0 + GROUP, (piece + 1) * step))
            queries, weights, sums = [], [], []
            for h in group:
                q = silu(q_ref[:, h * DH : (h + 1) * DH]).astype(BF16)
                k = silu(k_ref[:, columns(base + h * DH, 1)]).astype(BF16)
                s = lax.dot_general(q, k, (((1,), (1,)), ((), ())), preferred_element_type=F32)
                queries.append(q * joined)
                weights.append(s.astype(BF16) * allowed)
            for h, s in zip(group, weights):
                sums.append(jnp.dot(s, v_ref[:, columns(base + h * DH, 1)], preferred_element_type=F32))
            for n, h in enumerate(group):
                here = slice(h * DH, (h + 1) * DH)
                qm_ref[:, here] = queries[n]
                loc_ref[:, here] = sums[n]


def local_part(at, masks, q, k, v, offset, heads):
    rows = q.shape[0]
    width = heads * DH
    pieces = 4 if heads % 4 == 0 else 1
    return pl.pallas_call(
        functools.partial(local_kernel, offset, pieces),
        out_shape=[jax.ShapeDtypeStruct((rows, width), F32), jax.ShapeDtypeStruct((rows, width), BF16)],
        in_specs=[SMEM, VMEM, HBM, VMEM, VMEM],
        out_specs=[VMEM, VMEM],
        scratch_shapes=[pltpu.VMEM((rows, width), BF16), pltpu.SemaphoreType.DMA((pieces,))],
        compiler_params=PARAMS,
        cost_estimate=cost(4 * rows * rows * width, 12 * rows * width, 2 * rows * width),
    )(at, masks, in_hbm(q), k, v)


def attend(loc_ref, qm_ref, p_refs, att_ref):
    total = jnp.zeros((att_ref.shape[0], DH), F32)
    h = 0
    for p_ref in p_refs:
        for n in range(p_ref.shape[0]):
            cols = slice(h * DH, (h + 1) * DH)
            att = loc_ref[:, cols] + jnp.dot(qm_ref[:, cols], p_ref[n], preferred_element_type=F32)
            att = att.astype(BF16)
            att_ref[:, cols] = att
            wide = att.astype(F32)
            total = total + wide * wide
            h += 1
    return total


def first_kernel(loc_ref, qm_ref, pa_ref, pb_ref, att_ref, sum_ref):
    sum_ref[...] = attend(loc_ref, qm_ref, [pa_ref, pb_ref], att_ref)


def last_kernel(pieces, at_ref, loc_ref, qm_ref, pa_ref, pb_ref, att0_ref, sum0_ref, gain_ref, out_ref, att_ref, done_ref, sems):
    half = att_ref.shape[1] // DH
    core = at_ref[0] % 2
    total = attend(loc_ref, qm_ref, [pa_ref, pb_ref], att_ref) + sum0_ref[...]
    width = 2 * half * DH
    scale = lax.rsqrt(jnp.sum(total, axis=1, keepdims=True) / width + 1e-5)
    step = half // pieces
    copies = []
    for part, src in enumerate((att0_ref, att_ref)):
        base = jnp.where(core == part, 0, half * DH)
        for piece in range(pieces):
            for h in range(piece * step, (piece + 1) * step):
                cols = slice(h * DH, (h + 1) * DH)
                gain = gain_ref[:, columns(base + h * DH, 1)]
                done_ref[part, :, cols] = (src[:, cols].astype(F32) * scale * gain).astype(BF16)
            cols = slice(piece * step * DH, (piece + 1) * step * DH)
            there = columns(base + piece * step * DH, step)
            copies.append(pltpu.make_async_copy(done_ref.at[part, :, cols], out_ref.at[:, there], sems.at[part, piece]))
            copies[-1].start()
    for copy in copies:
        copy.wait()


def scan_kernel(rows, hop, len_ref, at_ref, state_ref, came_ref, out_ref):
    last = (at_ref[0] + 1) * rows - 1
    adds = (at_ref[0] >= hop) & same_doc(len_ref, last - hop * rows, last)
    out_ref[...] = state_ref[...] + jnp.where(adds, came_ref[...], 0.0)


def round_kernel(state_ref, out_ref):
    out_ref[...] = state_ref[...].astype(BF16)


def scan(lens, at, masks, k, v):
    rows, width = k.shape
    heads = width // DH
    blocks = lax.axis_size("ctx") * lax.axis_size("head")
    axes = ("ctx", "head")
    state = states(at, masks, k, v, lambda a: 0, heads, F32)
    spec = pl.BlockSpec((1, DH, DH), lambda h: (h, 0, 0))
    common = dict(grid=(heads,), out_specs=spec, compiler_params=PARAMS)
    hop = 1
    while hop < blocks:
        came = lax.ppermute(state, axes, [(b, b + hop) for b in range(blocks - hop)])
        state = pl.pallas_call(
            functools.partial(scan_kernel, rows, hop),
            out_shape=jax.ShapeDtypeStruct(state.shape, F32),
            in_specs=[SMEM, SMEM, spec, spec],
            **common,
        )(lens, at, state, came)
        hop *= 2
    state = pl.pallas_call(round_kernel, out_shape=jax.ShapeDtypeStruct(state.shape, BF16), in_specs=[spec], **common)(state)
    return lax.ppermute(state, axes, [(b, b + 1) for b in range(blocks - 1)])


def finish_first(loc, qm, pa, pb):
    rows, width = loc.shape
    return pl.pallas_call(
        first_kernel,
        out_shape=[jax.ShapeDtypeStruct((rows, width), BF16), jax.ShapeDtypeStruct((rows, DH), F32)],
        in_specs=[VMEM] * 4,
        out_specs=[VMEM, VMEM],
        compiler_params=PARAMS,
        cost_estimate=cost(2 * rows * DH * width, 10 * rows * width),
    )(loc, qm, pa, pb)


def finish_last(at, loc, qm, pa, pb, att, total, gain):
    rows, half_width = loc.shape
    pieces = 4 if half_width % (4 * DH) == 0 else 1
    return pl.pallas_call(
        functools.partial(last_kernel, pieces),
        out_shape=jax.ShapeDtypeStruct((rows, 2 * half_width), BF16),
        in_specs=[SMEM] + [VMEM] * 7,
        out_specs=HBM,
        scratch_shapes=[
            pltpu.VMEM((rows, half_width), BF16),
            pltpu.VMEM((2, rows, half_width), BF16),
            pltpu.SemaphoreType.DMA((2, pieces)),
        ],
        compiler_params=PARAMS,
        cost_estimate=cost(2 * rows * DH * half_width, 12 * rows * half_width),
    )(at, loc, qm, pa, pb, att, total, gain.reshape(1, 2 * half_width))


def general(lens, at, q, k, v, gain):
    half = q.shape[1] // (2 * DH)
    cut = half // 2
    masks = masks_only(lens, at, q.shape[0])
    before = scan(lens, at, masks, k, v)
    loc0, qm0 = local_part(at, masks, q, k, v, lambda a: 0, half)
    loc1, qm1 = local_part(at, masks, q, k, v, lambda a: half * DH, half)
    att, total = finish_first(loc0, qm0, before[:cut], before[cut:half])
    return finish_last(at * 2, loc1, qm1, before[half : half + cut], before[half + cut :], att, total, gain)


def neighbours(lens, at, q, k, v, gain):
    rows, width = q.shape
    heads = width // DH
    half = heads // 2
    cut = half // 2
    ctx_parts = lax.axis_size("ctx")
    pair = [(0, 1), (1, 0), (2, 3), (3, 2)]
    across = [(0, 2), (2, 0), (1, 3), (3, 1)]
    onward = [(c, c + 1) for c in range(ctx_parts - 1)]
    chunk_a, chunk_b = (cut, DH, DH), (half - cut, DH, DH)

    def own_half(a):
        return a % 2 * half * DH

    def other_half(a):
        return (1 - a % 2) * half * DH

    theirs, w, masks, k_in, v_in = opening(lens, at, k, v, half)
    got = lax.ppermute(theirs, "head", pair)
    own = states(at, masks, k_in, v_in, own_half, half, BF16)
    a, b = small_call(chip_kernel, [w, own, got], [chunk_a, chunk_b])
    r1 = lax.ppermute(b, "head", across)
    r2 = lax.ppermute(a, "ctx", onward)
    loc0, qm0 = local_part(at, masks, q, k_in, v_in, own_half, half)
    r1, loc0 = lax.optimization_barrier((r1, loc0))
    p4 = small_call(carry_kernel, [w, b, r1], [chunk_b])
    r4 = lax.ppermute(p4, "ctx", onward)
    p4, r2 = lax.optimization_barrier((p4, r2))
    p3 = small_call(relay_kernel, [w, a, r2], [chunk_a])
    r3 = lax.ppermute(p3, "head", across)
    loc1, qm1 = local_part(at, masks, q, k_in, v_in, other_half, half)
    r4, loc1 = lax.optimization_barrier((r4, loc1))
    mine_b, send_b = small_call(functools.partial(join_kernel, cut, False), [r1, r4, w, own, got], [chunk_b] * 2)
    other_b = lax.ppermute(send_b, "head", pair)
    r3, mine_b = lax.optimization_barrier((r3, mine_b))
    mine_a, send_a = small_call(functools.partial(join_kernel, 0, True), [r3, r2, w, own, got], [chunk_a] * 2)
    other_a = lax.ppermute(send_a, "head", pair)
    att, total = finish_first(loc0, qm0, mine_a, mine_b)
    return finish_last(at, loc1, qm1, other_a, other_b, att, total, gain)


def per_device(queries, keys_in, values, doc_lengths, rms_gain):
    at = jnp.reshape(lax.axis_index(("ctx", "head")).astype(jnp.int32), (1,))
    plan = neighbours if lax.axis_size("head") == 4 else general
    return plan(doc_lengths, at, queries, keys_in, values, rms_gain)


def solution(mesh):
    return jax.shard_map(
        per_device,
        mesh=mesh,
        in_specs=(
            P(("groups", "ctx", "head"), None),
            P(("groups", "ctx", "head"), None),
            P(("groups", "ctx", "head"), None),
            P("groups"),
            P(),
        ),
        out_specs=P(("groups", "ctx", "head"), None),
        check_vma=False,
    )
```

```python
import functools
import jax
import jax.numpy as jnp
from jax import lax
from jax.experimental import pallas as pl
from jax.experimental.pallas import tpu as pltpu
from jax.sharding import PartitionSpec as P

DH = 128
F32, BF16 = jnp.float32, jnp.bfloat16
VMEM = pl.BlockSpec(memory_space=pltpu.VMEM)
SMEM = pl.BlockSpec(memory_space=pltpu.SMEM)
HBM = pl.BlockSpec(memory_space=pltpu.HBM)
PARAMS = pltpu.CompilerParams(vmem_limit_bytes=12 << 20)
W_OWN, W_GOT, W_NEXT, W_FAR, W_ON, IS_X1, IS_CORE1 = range(7)
KEEP, ALLOWED, JOINED = range(3)
GROUP = 4


def in_hbm(x):
    return pltpu.with_memory_space_constraint(x, pltpu.HBM)


def silu(x):
    half = x.astype(F32) * 0.5
    return half + half * jnp.tanh(half)


def doc_start(len_ref, position):
    start = jnp.zeros_like(position)
    end = jnp.int32(0)
    for doc in range(len_ref.shape[0]):
        end = end + len_ref[doc]
        start = jnp.where(position >= end, end, start)
    return start


def same_doc(len_ref, earlier, later):
    return doc_start(len_ref, later) <= earlier


def columns(start, heads):
    return pl.ds(pl.multiple_of(start, DH), heads * DH)


def cost(flops, nbytes, trans=0):
    return pl.CostEstimate(flops=flops, bytes_accessed=nbytes, transcendentals=trans)


def make_masks(len_ref, at, rows):
    first = at * rows
    i = lax.broadcasted_iota(jnp.int32, (rows, DH), 0)
    keep = i >= doc_start(len_ref, first + rows - 1) - first
    start = doc_start(len_ref, first + i)
    joined = start < first
    i = lax.broadcasted_iota(jnp.int32, (rows, rows), 0)
    j = lax.broadcasted_iota(jnp.int32, (rows, rows), 1)
    allowed = (j <= i) & (j >= doc_start(len_ref, first + i) - first)
    return [jnp.where(mask, 1.0, 0.0).astype(BF16) for mask in (keep, allowed, joined)]


def block_states(keep, k_ref, v_ref, t_refs, base, ready=None):
    slots = [t_ref.at[h] for t_ref in t_refs for h in range(t_ref.shape[0])]
    heads = len(slots)
    for h0 in range(0, heads, GROUP):
        group = range(h0, min(h0 + GROUP, heads))
        sums = []
        for h in group:
            if ready is not None:
                ready(h)
            cols = columns(base + h * DH, 1)
            k = silu(k_ref[:, cols]).astype(BF16) * keep
            sums.append(lax.dot_general(k, v_ref[:, cols], (((0,), (0,)), ((), ())), preferred_element_type=F32))
        for h, t in zip(group, sums):
            slots[h][...] = t.astype(slots[h].dtype)


def own_kernel(offset, at_ref, m_ref, k_ref, v_ref, t_ref):
    block_states(m_ref[KEEP], k_ref, v_ref, [t_ref], offset(at_ref[0]))


def opening_kernel(pieces, len_hbm, at_ref, k_hbm, v_hbm, ta_ref, tb_ref, w_ref, m_ref, k_ref, v_ref, len_ref, sems, len_sem):
    at = at_ref[0]
    core, x = at % 2, (at // 2) % 2
    half, rows = ta_ref.shape[0] + tb_ref.shape[0], k_ref.shape[0]
    len_copy = pltpu.make_async_copy(len_hbm, len_ref, len_sem)
    len_copy.start()
    theirs, mine = (1 - core) * half * DH, core * half * DH
    step = half // pieces
    copies = []
    for piece in range(pieces + 1):
        cols = columns(theirs + piece * step * DH, step) if piece < pieces else columns(mine, half)
        pairs = ((k_hbm, k_ref), (v_hbm, v_ref))
        copies.append([pltpu.make_async_copy(src.at[:, cols], dst.at[:, cols], sems.at[piece, n]) for n, (src, dst) in enumerate(pairs)])
        for copy in copies[-1]:
            copy.start()
    len_copy.wait()
    chip = (at - core) * rows
    whole = same_doc(len_ref, chip + rows - 1, chip + 2 * rows - 1)
    values = {
        W_OWN: (core == 1) | whole,
        W_GOT: (core == 0) | whole,
        W_NEXT: same_doc(len_ref, chip + 2 * rows - 1, chip + 4 * rows - 1),
        W_FAR: same_doc(len_ref, chip - 2 * rows - 1, chip - 1),
        W_ON: same_doc(len_ref, chip - 1, chip + rows - 1),
        IS_X1: x == 1,
        IS_CORE1: core == 1,
    }
    for row, value in values.items():
        w_ref[row : row + 1, :] = jnp.full((1, DH), jnp.where(value, 1.0, 0.0), F32)

    masks = make_masks(len_ref, at, rows)
    for n, mask in enumerate(masks):
        m_ref[n] = mask

    def ready(h):
        if h % step == 0:
            for copy in copies[h // step]:
                copy.wait()

    block_states(masks[KEEP], k_ref, v_ref, [ta_ref, tb_ref], theirs, ready)
    for copy in copies[pieces]:
        copy.wait()


def masks_kernel(rows, len_ref, at_ref, m_ref):
    for n, mask in enumerate(make_masks(len_ref, at_ref[0], rows)):
        m_ref[n] = mask


def masks_only(lens, at, rows):
    return pl.pallas_call(
        functools.partial(masks_kernel, rows),
        out_shape=jax.ShapeDtypeStruct((3, rows, DH), BF16),
        in_specs=[SMEM, SMEM],
        out_specs=VMEM,
        compiler_params=PARAMS,
        cost_estimate=cost(1 << 20, 6 * rows * DH),
    )(lens, at)


def opening(lens, at, k, v, half, cut):
    pieces = 4 if half % 4 == 0 else 1
    rows = k.shape[0]
    vmem = jax.ShapeDtypeStruct(k.shape, BF16)
    return pl.pallas_call(
        functools.partial(opening_kernel, pieces),
        out_shape=[
            jax.ShapeDtypeStruct((cut, DH, DH), BF16),
            jax.ShapeDtypeStruct((half - cut, DH, DH), BF16),
            jax.ShapeDtypeStruct((8, DH), F32),
            jax.ShapeDtypeStruct((3, rows, DH), BF16),
            vmem,
            vmem,
        ],
        in_specs=[HBM, SMEM, HBM, HBM],
        out_specs=[VMEM] * 6,
        scratch_shapes=[pltpu.SMEM(lens.shape, jnp.int32), pltpu.SemaphoreType.DMA((pieces + 1, 2)), pltpu.SemaphoreType.DMA],
        compiler_params=PARAMS,
        cost_estimate=cost(2 * half * rows * DH * DH, 4 * k.size, half * rows * DH),
    )(in_hbm(lens), at, in_hbm(k), in_hbm(v))


def states(at, masks, k, v, offset, heads, dtype):
    rows = k.shape[0]
    return pl.pallas_call(
        functools.partial(own_kernel, offset),
        out_shape=jax.ShapeDtypeStruct((heads, DH, DH), dtype),
        in_specs=[SMEM, VMEM, VMEM, VMEM],
        out_specs=VMEM,
        compiler_params=PARAMS,
        cost_estimate=cost(2 * heads * rows * DH * DH, heads * DH * (4 * rows + 2 * DH), heads * rows * DH),
    )(at, masks, k, v)


def weight(w_ref, row):
    return jnp.broadcast_to(w_ref[row : row + 1, :], (DH, DH)).astype(BF16)


def chip_kernel(start, w_ref, own_ref, got_ref, chip_ref):
    w_own, w_got = weight(w_ref, W_OWN), weight(w_ref, W_GOT)
    for h in range(chip_ref.shape[0]):
        chip_ref[h] = own_ref[start + h] * w_own + got_ref[h] * w_got


def relay_kernel(w_ref, a_ref, r2_ref, p3_ref):
    is_x1 = weight(w_ref, IS_X1)
    is_x0 = 1.0 - is_x1
    for h in range(p3_ref.shape[0]):
        p3_ref[h] = r2_ref[h] * is_x1 + a_ref[h] * is_x0


def carry_kernel(w_ref, b_ref, r1_ref, p4_ref):
    is_x1, w_next = weight(w_ref, IS_X1), weight(w_ref, W_NEXT)
    w_r = 1.0 - is_x1
    w_b = is_x1 + w_r * w_next
    for h in range(p4_ref.shape[0]):
        p4_ref[h] = b_ref[h] * w_b + r1_ref[h] * w_r


def join_kernel(start, first_row, near_ref, far_ref, w_ref, own_ref, got_ref, mine_ref, send_ref):
    w, on, is_x1, core1 = (weight(w_ref, row) for row in (W_FAR, W_ON, IS_X1, IS_CORE1))
    core0 = 1.0 - core1
    if first_row:
        w_near = None
    else:
        w_near = is_x1
        w = is_x1 * w + (1.0 - is_x1)
    m1, m2 = core1 * on + core0, core0 * on + core1
    for h in range(mine_ref.shape[0]):
        near = near_ref[h] if w_near is None else near_ref[h] * w_near
        p = near + far_ref[h] * w
        mine_ref[h] = p * m1 + got_ref[h] * core1
        send_ref[h] = p * m2 + own_ref[start + h] * core0


def small_call(kernel, ins, outs):
    many = len(outs) > 1
    shapes = [jax.ShapeDtypeStruct(s, BF16) for s in outs]
    return pl.pallas_call(
        kernel,
        out_shape=shapes if many else shapes[0],
        in_specs=[VMEM] * len(ins),
        out_specs=[VMEM] * len(outs) if many else VMEM,
        compiler_params=PARAMS,
        cost_estimate=cost(1 << 20, 1 << 20),
    )(*ins)


def local_kernel(offset, pieces, at_ref, m_ref, q_hbm, k_ref, v_ref, loc_ref, qm_ref, q_ref, sems):
    heads = loc_ref.shape[1] // DH
    base = offset(at_ref[0])
    step = heads // pieces
    copies = []
    for piece in range(pieces):
        here = slice(piece * step * DH, (piece + 1) * step * DH)
        copies.append(pltpu.make_async_copy(q_hbm.at[:, columns(base + piece * step * DH, step)], q_ref.at[:, here], sems.at[piece]))
        copies[-1].start()
    allowed, joined = m_ref[ALLOWED], m_ref[JOINED]
    for piece in range(pieces):
        copies[piece].wait()
        for h0 in range(piece * step, (piece + 1) * step, GROUP):
            group = range(h0, min(h0 + GROUP, (piece + 1) * step))
            queries, weights, sums = [], [], []
            for h in group:
                q = silu(q_ref[:, h * DH : (h + 1) * DH]).astype(BF16)
                k = silu(k_ref[:, columns(base + h * DH, 1)]).astype(BF16)
                s = lax.dot_general(q, k, (((1,), (1,)), ((), ())), preferred_element_type=F32)
                queries.append(q * joined)
                weights.append(s.astype(BF16) * allowed)
            for h, s in zip(group, weights):
                sums.append(jnp.dot(s, v_ref[:, columns(base + h * DH, 1)], preferred_element_type=F32))
            for n, h in enumerate(group):
                here = slice(h * DH, (h + 1) * DH)
                qm_ref[:, here] = queries[n]
                loc_ref[:, here] = sums[n]


def local_part(at, masks, q, k, v, offset, heads):
    rows = q.shape[0]
    width = heads * DH
    pieces = 4 if heads % 4 == 0 else 1
    return pl.pallas_call(
        functools.partial(local_kernel, offset, pieces),
        out_shape=[jax.ShapeDtypeStruct((rows, width), F32), jax.ShapeDtypeStruct((rows, width), BF16)],
        in_specs=[SMEM, VMEM, HBM, VMEM, VMEM],
        out_specs=[VMEM, VMEM],
        scratch_shapes=[pltpu.VMEM((rows, width), BF16), pltpu.SemaphoreType.DMA((pieces,))],
        compiler_params=PARAMS,
        cost_estimate=cost(0, 0),
    )(at, masks, in_hbm(q), k, v)


def attend(loc_ref, qm_ref, p_ref, start, att_ref):
    total = jnp.zeros((att_ref.shape[0], DH), F32)
    heads = p_ref.shape[0]
    for h0 in range(0, heads, GROUP):
        sums = []
        group = range(h0, min(h0 + GROUP, heads))
        for h in group:
            cols = slice((start + h) * DH, (start + h + 1) * DH)
            att = loc_ref[:, cols] + jnp.dot(qm_ref[:, cols], p_ref[h], preferred_element_type=F32)
            sums.append(att.astype(BF16))
        for h, att in zip(group, sums):
            att_ref[:, h * DH : (h + 1) * DH] = att
            wide = att.astype(F32)
            total = total + wide * wide
    return total


def first_kernel(starts, *refs):
    n = len(starts)
    ins, outs = refs[: 3 * n], refs[3 * n :]
    total = 0.0
    for c, start in enumerate(starts):
        total = total + attend(*ins[3 * c : 3 * c + 3], start, outs[c])
    outs[n][...] = total


def last_kernel(start, loc_ref, qm_ref, p_ref, at_ref, gain_ref, sum_ref, own_a_ref, own_b_ref, other_b_ref, out_ref, att_ref, done_ref, sems):
    half = loc_ref.shape[1] // DH
    cut = p_ref.shape[0]
    core = at_ref[0] % 2
    total = attend(loc_ref, qm_ref, p_ref, start, att_ref) + sum_ref[...]
    width = 2 * half * DH
    scale = lax.rsqrt(jnp.sum(total, axis=1, keepdims=True) / width + 1e-5)
    scale = jnp.broadcast_to(scale, (att_ref.shape[0], DH))
    own, other = core * half * DH, (1 - core) * half * DH
    copies = []
    parts = ((own_a_ref, own), (own_b_ref, own + cut * DH), (other_b_ref, other + cut * DH), (att_ref, other))
    for n, (src, base) in enumerate(parts):
        heads = src.shape[1] // DH
        for h in range(heads):
            cols = slice(h * DH, (h + 1) * DH)
            gain = gain_ref[:, columns(base + h * DH, 1)]
            done_ref[n, :, cols] = (src[:, cols].astype(F32) * scale * gain).astype(BF16)
        copies.append(pltpu.make_async_copy(done_ref.at[n, :, : heads * DH], out_ref.at[:, columns(base, heads)], sems.at[n]))
        copies[-1].start()
    for copy in copies:
        copy.wait()


def scan_kernel(rows, hop, len_ref, at_ref, state_ref, came_ref, out_ref):
    last = (at_ref[0] + 1) * rows - 1
    adds = (at_ref[0] >= hop) & same_doc(len_ref, last - hop * rows, last)
    out_ref[...] = state_ref[...] + jnp.where(adds, came_ref[...], 0.0)


def round_kernel(state_ref, out_ref):
    out_ref[...] = state_ref[...].astype(BF16)


def scan(lens, at, masks, k, v):
    rows, width = k.shape
    heads = width // DH
    blocks = lax.axis_size("ctx") * lax.axis_size("head")
    axes = ("ctx", "head")
    state = states(at, masks, k, v, lambda a: 0, heads, F32)
    spec = pl.BlockSpec((1, DH, DH), lambda h: (h, 0, 0))
    common = dict(grid=(heads,), out_specs=spec, compiler_params=PARAMS)
    hop = 1
    while hop < blocks:
        came = lax.ppermute(state, axes, [(b, b + hop) for b in range(blocks - hop)])
        state = pl.pallas_call(
            functools.partial(scan_kernel, rows, hop),
            out_shape=jax.ShapeDtypeStruct(state.shape, F32),
            in_specs=[SMEM, SMEM, spec, spec],
            **common,
        )(lens, at, state, came)
        hop *= 2
    state = pl.pallas_call(round_kernel, out_shape=jax.ShapeDtypeStruct(state.shape, BF16), in_specs=[spec], **common)(state)
    return lax.ppermute(state, axes, [(b, b + 1) for b in range(blocks - 1)])


def finish_first(chunks):
    rows = chunks[0][0].shape[0]
    ins = [x for chunk in chunks for x in chunk[:3]]
    shapes = [jax.ShapeDtypeStruct((rows, chunk[2].shape[0] * DH), BF16) for chunk in chunks]
    return pl.pallas_call(
        functools.partial(first_kernel, tuple(chunk[3] for chunk in chunks)),
        out_shape=shapes + [jax.ShapeDtypeStruct((rows, DH), F32)],
        in_specs=[VMEM] * len(ins),
        out_specs=[VMEM] * (len(shapes) + 1),
        compiler_params=PARAMS,
        cost_estimate=cost(2 * rows * DH * DH * 16, 1 << 21),
    )(*ins)


def finish_last(at, chunk, gain, own_a, own_b, other_b, total):
    loc, qm, p, start = chunk
    rows, half_width = loc.shape
    widest = max(own_a.shape[1], own_b.shape[1])
    return pl.pallas_call(
        functools.partial(last_kernel, start),
        out_shape=jax.ShapeDtypeStruct((rows, 2 * half_width), BF16),
        in_specs=[VMEM] * 3 + [SMEM] + [VMEM] * 5,
        out_specs=HBM,
        scratch_shapes=[
            pltpu.VMEM((rows, p.shape[0] * DH), BF16),
            pltpu.VMEM((4, rows, widest), BF16),
            pltpu.SemaphoreType.DMA((4,)),
        ],
        compiler_params=PARAMS,
        cost_estimate=cost(2 * rows * DH * half_width, 12 * rows * half_width),
    )(loc, qm, p, at, gain.reshape(1, 2 * half_width), total, own_a, own_b, other_b)


def general(lens, at, q, k, v, gain):
    half = q.shape[1] // (2 * DH)
    cut = half // 2
    masks = masks_only(lens, at, q.shape[0])
    before = scan(lens, at, masks, k, v)
    loc0, qm0 = local_part(at, masks, q, k, v, lambda a: 0, half)
    loc1, qm1 = local_part(at, masks, q, k, v, lambda a: half * DH, half)
    first = finish_first([(loc0, qm0, before[:cut], 0), (loc0, qm0, before[cut:half], cut), (loc1, qm1, before[half + cut :], cut)])
    return finish_last(at * 2, (loc1, qm1, before[half : half + cut], 0), gain, *first)


def neighbours(lens, at, q, k, v, gain):
    rows, width = q.shape
    heads = width // DH
    half = heads // 2
    cut = half // 2
    ctx_parts = lax.axis_size("ctx")
    pair = [(0, 1), (1, 0), (2, 3), (3, 2)]
    across = [(0, 2), (2, 0), (1, 3), (3, 1)]
    onward = [(c, c + 1) for c in range(ctx_parts - 1)]
    chunk_a, chunk_b = (cut, DH, DH), (half - cut, DH, DH)

    def own_half(a):
        return a % 2 * half * DH

    def other_half(a):
        return (1 - a % 2) * half * DH

    theirs_a, theirs_b, w, masks, k_in, v_in = opening(lens, at, k, v, half, cut)
    got_b = lax.ppermute(theirs_b, "head", pair)
    got_a = lax.ppermute(theirs_a, "head", pair)
    own = states(at, masks, k_in, v_in, own_half, half, BF16)
    b = small_call(functools.partial(chip_kernel, cut), [w, own, got_b], [chunk_b])
    r1 = lax.ppermute(b, "head", across)
    a = small_call(functools.partial(chip_kernel, 0), [w, own, got_a], [chunk_a])
    r2 = lax.ppermute(a, "ctx", onward)
    a, masks = lax.optimization_barrier((a, masks))
    loc0, qm0 = local_part(at, masks, q, k_in, v_in, own_half, half)
    r1, loc0 = lax.optimization_barrier((r1, loc0))
    p4 = small_call(carry_kernel, [w, b, r1], [chunk_b])
    r4 = lax.ppermute(p4, "ctx", onward)
    p4, r2 = lax.optimization_barrier((p4, r2))
    p3 = small_call(relay_kernel, [w, a, r2], [chunk_a])
    r3 = lax.ppermute(p3, "head", across)
    p3, masks = lax.optimization_barrier((p3, masks))
    loc1, qm1 = local_part(at, masks, q, k_in, v_in, other_half, half)
    r4, loc1 = lax.optimization_barrier((r4, loc1))
    mine_b, send_b = small_call(functools.partial(join_kernel, cut, False), [r1, r4, w, own, got_b], [chunk_b] * 2)
    other_b = lax.ppermute(send_b, "head", pair)
    r3, other_b = lax.optimization_barrier((r3, other_b))
    mine_a, send_a = small_call(functools.partial(join_kernel, 0, True), [r3, r2, w, own, got_a], [chunk_a] * 2)
    other_a = lax.ppermute(send_a, "head", pair)
    first = finish_first([(loc0, qm0, mine_a, 0), (loc0, qm0, mine_b, cut), (loc1, qm1, other_b, cut)])
    return finish_last(at, (loc1, qm1, other_a, 0), gain, *first)


def per_device(queries, keys_in, values, doc_lengths, rms_gain):
    at = jnp.reshape(lax.axis_index(("ctx", "head")).astype(jnp.int32), (1,))
    plan = neighbours if lax.axis_size("head") == 4 else general
    return plan(doc_lengths, at, queries, keys_in, values, rms_gain)


def solution(mesh):
    return jax.shard_map(
        per_device,
        mesh=mesh,
        in_specs=(
            P(("groups", "ctx", "head"), None),
            P(("groups", "ctx", "head"), None),
            P(("groups", "ctx", "head"), None),
            P("groups"),
            P(),
        ),
        out_specs=P(("groups", "ctx", "head"), None),
        check_vma=False,
    )
```

```python
import functools
import jax
import jax.numpy as jnp
from jax import lax
from jax.experimental import pallas as pl
from jax.experimental.pallas import tpu as pltpu
from jax.sharding import PartitionSpec as P

DH = 128
F32, BF16 = jnp.float32, jnp.bfloat16
VMEM = pl.BlockSpec(memory_space=pltpu.VMEM)
SMEM = pl.BlockSpec(memory_space=pltpu.SMEM)
HBM = pl.BlockSpec(memory_space=pltpu.HBM)
PARAMS = pltpu.CompilerParams(vmem_limit_bytes=12 << 20)
W_OWN, W_GOT, W_NEXT, W_FAR, W_ON, IS_X1, IS_CORE1, IS_ODD = range(8)
KEEP, ALLOWED, JOINED = range(3)
GROUP = 4


def in_hbm(x):
    return pltpu.with_memory_space_constraint(x, pltpu.HBM)


def silu(x):
    half = x.astype(F32) * 0.5
    return half + half * jnp.tanh(half)


def doc_start(len_ref, position):
    start = jnp.zeros_like(position)
    end = jnp.int32(0)
    for doc in range(len_ref.shape[0]):
        end = end + len_ref[doc]
        start = jnp.where(position >= end, end, start)
    return start


def same_doc(len_ref, earlier, later):
    return doc_start(len_ref, later) <= earlier


def columns(start, heads):
    return pl.ds(pl.multiple_of(start, DH), heads * DH)


def cost(flops, nbytes, trans=0):
    return pl.CostEstimate(flops=flops, bytes_accessed=nbytes, transcendentals=trans)


def make_masks(len_ref, at, rows):
    first = at * rows
    i = lax.broadcasted_iota(jnp.int32, (rows, DH), 0)
    keep = i >= doc_start(len_ref, first + rows - 1) - first
    start = doc_start(len_ref, first + i)
    joined = start < first
    i = lax.broadcasted_iota(jnp.int32, (rows, rows), 0)
    j = lax.broadcasted_iota(jnp.int32, (rows, rows), 1)
    allowed = (j <= i) & (j >= doc_start(len_ref, first + i) - first)
    return [jnp.where(mask, 1.0, 0.0).astype(BF16) for mask in (keep, allowed, joined)]


def block_states(keep, k_ref, v_ref, t_refs, base, ready=None):
    slots = [t_ref.at[h] for t_ref in t_refs for h in range(t_ref.shape[0])]
    heads = len(slots)
    for h0 in range(0, heads, GROUP):
        group = range(h0, min(h0 + GROUP, heads))
        sums = []
        for h in group:
            if ready is not None:
                ready(h)
            cols = columns(base + h * DH, 1)
            k = silu(k_ref[:, cols]).astype(BF16) * keep
            sums.append(lax.dot_general(k, v_ref[:, cols], (((0,), (0,)), ((), ())), preferred_element_type=F32))
        for h, t in zip(group, sums):
            slots[h][...] = t.astype(slots[h].dtype)


def own_kernel(offset, at_ref, m_ref, k_ref, v_ref, t_ref):
    block_states(m_ref[KEEP], k_ref, v_ref, [t_ref], offset(at_ref[0]))


def opening_kernel(start, pieces, len_hbm, at_ref, k_hbm, v_hbm, t_ref, w_ref, m_ref, k_ref, v_ref, len_ref, sems, len_sem):
    at = at_ref[0]
    core, x = at % 2, (at // 2) % 2
    heads, rows = t_ref.shape[0], k_ref.shape[0]
    len_copy = pltpu.make_async_copy(len_hbm, len_ref, len_sem)
    len_copy.start()
    base = start(at)
    step = heads // pieces
    copies = []
    for piece in range(pieces):
        there, here = columns(base + piece * step * DH, step), slice(piece * step * DH, (piece + 1) * step * DH)
        pairs = ((k_hbm, k_ref), (v_hbm, v_ref))
        copies.append([pltpu.make_async_copy(src.at[:, there], dst.at[:, here], sems.at[piece, n]) for n, (src, dst) in enumerate(pairs)])
        for copy in copies[-1]:
            copy.start()
    len_copy.wait()
    chip = (at - core) * rows
    whole = same_doc(len_ref, chip + rows - 1, chip + 2 * rows - 1)
    values = {
        W_OWN: (core == 1) | whole,
        W_GOT: (core == 0) | whole,
        W_NEXT: same_doc(len_ref, chip + 2 * rows - 1, chip + 4 * rows - 1),
        W_FAR: same_doc(len_ref, chip - 2 * rows - 1, chip - 1),
        W_ON: same_doc(len_ref, chip - 1, chip + rows - 1),
        IS_X1: x == 1,
        IS_CORE1: core == 1,
        IS_ODD: (at // 4) % 2 == 1,
    }
    for row, value in values.items():
        w_ref[row : row + 1, :] = jnp.full((1, DH), jnp.where(value, 1.0, 0.0), F32)
    masks = make_masks(len_ref, at, rows)
    for n, mask in enumerate(masks):
        m_ref[n] = mask

    def ready(h):
        if h % step == 0:
            for copy in copies[h // step]:
                copy.wait()

    block_states(masks[KEEP], k_ref, v_ref, [t_ref], 0, ready)


def masks_kernel(rows, len_ref, at_ref, m_ref):
    for n, mask in enumerate(make_masks(len_ref, at_ref[0], rows)):
        m_ref[n] = mask


def masks_only(lens, at, rows):
    return pl.pallas_call(
        functools.partial(masks_kernel, rows),
        out_shape=jax.ShapeDtypeStruct((3, rows, DH), BF16),
        in_specs=[SMEM, SMEM],
        out_specs=VMEM,
        compiler_params=PARAMS,
        cost_estimate=cost(1 << 20, 6 * rows * DH),
    )(lens, at)


def opening(lens, at, k, v, start, heads):
    pieces = 1
    rows = k.shape[0]
    return pl.pallas_call(
        functools.partial(opening_kernel, start, pieces),
        out_shape=[
            jax.ShapeDtypeStruct((heads, DH, DH), BF16),
            jax.ShapeDtypeStruct((8, DH), F32),
            jax.ShapeDtypeStruct((3, rows, DH), BF16),
        ],
        in_specs=[HBM, SMEM, HBM, HBM],
        out_specs=[VMEM] * 3,
        scratch_shapes=[
            pltpu.VMEM((rows, heads * DH), BF16),
            pltpu.VMEM((rows, heads * DH), BF16),
            pltpu.SMEM(lens.shape, jnp.int32),
            pltpu.SemaphoreType.DMA((pieces, 2)),
            pltpu.SemaphoreType.DMA,
        ],
        compiler_params=PARAMS,
        cost_estimate=cost(2 * heads * rows * DH * DH, 4 * rows * heads * DH, heads * rows * DH),
    )(in_hbm(lens), at, in_hbm(k), in_hbm(v))


def rest_kernel(half, at_ref, m_ref, k_ref, v_ref, ta_ref, own_ref):
    core = at_ref[0] % 2
    block_states(m_ref[KEEP], k_ref, v_ref, [own_ref], core * half * DH)
    block_states(m_ref[KEEP], k_ref, v_ref, [ta_ref], (1 - core) * half * DH)


def rest_states(at, masks, k, v, half, cut):
    return pl.pallas_call(
        functools.partial(rest_kernel, half),
        out_shape=[jax.ShapeDtypeStruct((cut, DH, DH), BF16), jax.ShapeDtypeStruct((half, DH, DH), BF16)],
        in_specs=[SMEM, VMEM, VMEM, VMEM],
        out_specs=[VMEM, VMEM],
        compiler_params=PARAMS,
        cost_estimate=cost(0, 0),
    )(at, masks, k, v)


def states(at, masks, k, v, offset, heads, dtype):
    rows = k.shape[0]
    return pl.pallas_call(
        functools.partial(own_kernel, offset),
        out_shape=jax.ShapeDtypeStruct((heads, DH, DH), dtype),
        in_specs=[SMEM, VMEM, VMEM, VMEM],
        out_specs=VMEM,
        compiler_params=PARAMS,
        cost_estimate=cost(2 * heads * rows * DH * DH, heads * DH * (4 * rows + 2 * DH), heads * rows * DH),
    )(at, masks, k, v)


def weight(w_ref, row):
    return jnp.broadcast_to(w_ref[row : row + 1, :], (DH, DH)).astype(BF16)


def chip_kernel(start, w_ref, own_ref, got_ref, chip_ref):
    w_own, w_got = weight(w_ref, W_OWN), weight(w_ref, W_GOT)
    for h in range(chip_ref.shape[0]):
        chip_ref[h] = own_ref[start + h] * w_own + got_ref[h] * w_got


def came(w_ref, odd_ref, even_ref, h):
    odd = weight(w_ref, IS_ODD)
    return odd_ref[h] * odd + even_ref[h] * (1.0 - odd)


def relay_kernel(w_ref, a_ref, odd_ref, even_ref, p3_ref, r2_ref):
    is_x1 = weight(w_ref, IS_X1)
    is_x0 = 1.0 - is_x1
    for h in range(p3_ref.shape[0]):
        r2 = came(w_ref, odd_ref, even_ref, h)
        r2_ref[h] = r2
        p3_ref[h] = r2 * is_x1 + a_ref[h] * is_x0


def carry_kernel(w_ref, b_ref, r1_ref, p4_ref):
    is_x1, w_next = weight(w_ref, IS_X1), weight(w_ref, W_NEXT)
    w_r = 1.0 - is_x1
    w_b = is_x1 + w_r * w_next
    for h in range(p4_ref.shape[0]):
        p4_ref[h] = b_ref[h] * w_b + r1_ref[h] * w_r


def join(w_ref, p, own, got, mine_ref, send_ref, h):
    on, core1 = weight(w_ref, W_ON), weight(w_ref, IS_CORE1)
    core0 = 1.0 - core1
    mine_ref[h] = p * (core1 * on + core0) + got * core1
    send_ref[h] = p * (core0 * on + core1) + own * core0


def join_a_kernel(w_ref, r3_ref, r2_ref, own_ref, got_ref, mine_ref, send_ref):
    far = weight(w_ref, W_FAR)
    for h in range(mine_ref.shape[0]):
        join(w_ref, r3_ref[h] + r2_ref[h] * far, own_ref[h], got_ref[h], mine_ref, send_ref, h)


def join_b_kernel(start, w_ref, r1_ref, odd_ref, even_ref, own_ref, got_ref, mine_ref, send_ref):
    is_x1 = weight(w_ref, IS_X1)
    far = is_x1 * weight(w_ref, W_FAR) + (1.0 - is_x1)
    for h in range(mine_ref.shape[0]):
        p = r1_ref[h] * is_x1 + came(w_ref, odd_ref, even_ref, h) * far
        join(w_ref, p, own_ref[start + h], got_ref[h], mine_ref, send_ref, h)


def small_call(kernel, ins, outs):
    many = len(outs) > 1
    shapes = [jax.ShapeDtypeStruct(s, BF16) for s in outs]
    return pl.pallas_call(
        kernel,
        out_shape=shapes if many else shapes[0],
        in_specs=[VMEM] * len(ins),
        out_specs=[VMEM] * len(outs) if many else VMEM,
        compiler_params=PARAMS,
        cost_estimate=cost(1 << 20, 1 << 20),
    )(*ins)


def local_kernel(offset, pieces, at_ref, m_ref, q_hbm, k_ref, v_ref, loc_ref, qm_ref, q_ref, sems):
    heads = loc_ref.shape[1] // DH
    base = offset(at_ref[0])
    step = heads // pieces
    copies = []
    for piece in range(pieces):
        here = slice(piece * step * DH, (piece + 1) * step * DH)
        copies.append(pltpu.make_async_copy(q_hbm.at[:, columns(base + piece * step * DH, step)], q_ref.at[:, here], sems.at[piece]))
        copies[-1].start()
    allowed, joined = m_ref[ALLOWED], m_ref[JOINED]
    for piece in range(pieces):
        copies[piece].wait()
        for h0 in range(piece * step, (piece + 1) * step, GROUP):
            group = range(h0, min(h0 + GROUP, (piece + 1) * step))
            queries, weights, sums = [], [], []
            for h in group:
                q = silu(q_ref[:, h * DH : (h + 1) * DH]).astype(BF16)
                k = silu(k_ref[:, columns(base + h * DH, 1)]).astype(BF16)
                s = lax.dot_general(q, k, (((1,), (1,)), ((), ())), preferred_element_type=F32)
                queries.append(q * joined)
                weights.append(s.astype(BF16) * allowed)
            for h, s in zip(group, weights):
                sums.append(jnp.dot(s, v_ref[:, columns(base + h * DH, 1)], preferred_element_type=F32))
            for n, h in enumerate(group):
                here = slice(h * DH, (h + 1) * DH)
                qm_ref[:, here] = queries[n]
                loc_ref[:, here] = sums[n]


def local_part(at, masks, q, k, v, offset, heads):
    rows = q.shape[0]
    width = heads * DH
    pieces = 4 if heads % 4 == 0 else 1
    return pl.pallas_call(
        functools.partial(local_kernel, offset, pieces),
        out_shape=[jax.ShapeDtypeStruct((rows, width), F32), jax.ShapeDtypeStruct((rows, width), BF16)],
        in_specs=[SMEM, VMEM, HBM, VMEM, VMEM],
        out_specs=[VMEM, VMEM],
        scratch_shapes=[pltpu.VMEM((rows, width), BF16), pltpu.SemaphoreType.DMA((pieces,))],
        compiler_params=PARAMS,
        cost_estimate=cost(0, 0),
    )(at, masks, in_hbm(q), k, v)


def attend(loc_ref, qm_ref, p_ref, start, gain_ref, base, out_ref):
    total = jnp.zeros((out_ref.shape[0], DH), F32)
    heads = p_ref.shape[0]
    for h0 in range(0, heads, GROUP):
        sums = []
        group = range(h0, min(h0 + GROUP, heads))
        for h in group:
            cols = slice((start + h) * DH, (start + h + 1) * DH)
            att = loc_ref[:, cols] + jnp.dot(qm_ref[:, cols], p_ref[h], preferred_element_type=F32)
            sums.append(att.astype(BF16).astype(F32))
        for h, att in zip(group, sums):
            out_ref[:, h * DH : (h + 1) * DH] = att * gain_ref[:, columns(base + h * DH, 1)]
            total = total + att * att
    return total


def bases(at, starts, half):
    own, other = at % 2 * half * DH, (1 - at % 2) * half * DH
    return [(own if n < 2 else other) + start * DH for n, start in enumerate(starts)]


def first_kernel(starts, at_ref, gain_ref, *refs):
    n = len(starts)
    ins, outs = refs[: 3 * n], refs[3 * n :]
    total = 0.0
    for c, base in enumerate(bases(at_ref[0], starts, ins[0].shape[1] // DH)):
        total = total + attend(*ins[3 * c : 3 * c + 3], starts[c], gain_ref, base, outs[c])
    outs[n][...] = total


def last_kernel(starts, at_ref, gain_ref, loc_ref, qm_ref, p_ref, sum_ref, c0_ref, c1_ref, c2_ref, out_ref, c3_ref, done_ref, sems):
    half = loc_ref.shape[1] // DH
    there = bases(at_ref[0], starts, half)
    total = attend(loc_ref, qm_ref, p_ref, starts[3], gain_ref, there[3], c3_ref) + sum_ref[...]
    width = 2 * half * DH
    scale = lax.rsqrt(jnp.sum(total, axis=1, keepdims=True) / width + 1e-5)
    scale = jnp.broadcast_to(scale, (c3_ref.shape[0], DH))
    copies = []
    for n, src in enumerate((c0_ref, c1_ref, c2_ref, c3_ref)):
        heads = src.shape[1] // DH
        for h in range(heads):
            cols = slice(h * DH, (h + 1) * DH)
            done_ref[n, :, cols] = (src[:, cols] * scale).astype(BF16)
        copies.append(pltpu.make_async_copy(done_ref.at[n, :, : heads * DH], out_ref.at[:, columns(there[n], heads)], sems.at[n]))
        copies[-1].start()
    for copy in copies:
        copy.wait()


def scan_kernel(rows, hop, len_ref, at_ref, state_ref, came_ref, out_ref):
    last = (at_ref[0] + 1) * rows - 1
    adds = (at_ref[0] >= hop) & same_doc(len_ref, last - hop * rows, last)
    out_ref[...] = state_ref[...] + jnp.where(adds, came_ref[...], 0.0)


def round_kernel(state_ref, out_ref):
    out_ref[...] = state_ref[...].astype(BF16)


def scan(lens, at, masks, k, v):
    rows, width = k.shape
    heads = width // DH
    blocks = lax.axis_size("ctx") * lax.axis_size("head")
    axes = ("ctx", "head")
    state = states(at, masks, k, v, lambda a: 0, heads, F32)
    spec = pl.BlockSpec((1, DH, DH), lambda h: (h, 0, 0))
    common = dict(grid=(heads,), out_specs=spec, compiler_params=PARAMS)
    hop = 1
    while hop < blocks:
        came = lax.ppermute(state, axes, [(b, b + hop) for b in range(blocks - hop)])
        state = pl.pallas_call(
            functools.partial(scan_kernel, rows, hop),
            out_shape=jax.ShapeDtypeStruct(state.shape, F32),
            in_specs=[SMEM, SMEM, spec, spec],
            **common,
        )(lens, at, state, came)
        hop *= 2
    state = pl.pallas_call(round_kernel, out_shape=jax.ShapeDtypeStruct(state.shape, BF16), in_specs=[spec], **common)(state)
    return lax.ppermute(state, axes, [(b, b + 1) for b in range(blocks - 1)])


def finish(at, gain, chunks):
    rows, half_width = chunks[0][0].shape
    gain = gain.reshape(1, 2 * half_width)
    starts = tuple(chunk[3] for chunk in chunks)
    ins = [x for chunk in chunks[:-1] for x in chunk[:3]]
    shapes = [jax.ShapeDtypeStruct((rows, chunk[2].shape[0] * DH), F32) for chunk in chunks[:-1]]
    *parts, total = pl.pallas_call(
        functools.partial(first_kernel, starts[:-1]),
        out_shape=shapes + [jax.ShapeDtypeStruct((rows, DH), F32)],
        in_specs=[SMEM] + [VMEM] * (1 + len(ins)),
        out_specs=[VMEM] * (len(shapes) + 1),
        compiler_params=PARAMS,
        cost_estimate=cost(3 * rows * DH * half_width, 1 << 21),
    )(at, gain, *ins)
    last = chunks[-1]
    return pl.pallas_call(
        functools.partial(last_kernel, starts),
        out_shape=jax.ShapeDtypeStruct((rows, 2 * half_width), BF16),
        in_specs=[SMEM] + [VMEM] * (5 + len(parts)),
        out_specs=HBM,
        scratch_shapes=[
            pltpu.VMEM((rows, last[2].shape[0] * DH), F32),
            pltpu.VMEM((4, rows, max(chunk[2].shape[0] for chunk in chunks) * DH), BF16),
            pltpu.SemaphoreType.DMA((4,)),
        ],
        compiler_params=PARAMS,
        cost_estimate=cost(2 * rows * DH * half_width, 12 * rows * half_width),
    )(at, gain, *last[:3], total, *parts)


def general(lens, at, q, k, v, gain):
    half = q.shape[1] // (2 * DH)
    cut = half // 2
    masks = masks_only(lens, at, q.shape[0])
    before = scan(lens, at, masks, k, v)
    loc0, qm0 = local_part(at, masks, q, k, v, lambda a: 0, half)
    loc1, qm1 = local_part(at, masks, q, k, v, lambda a: half * DH, half)
    chunks = [(loc0, qm0, before[:cut], 0), (loc0, qm0, before[cut:half], cut)]
    chunks += [(loc1, qm1, before[half + cut :], cut), (loc1, qm1, before[half : half + cut], 0)]
    return finish(at * 2, gain, chunks)


def neighbours(lens, at, q, k, v, gain):
    rows, width = q.shape
    heads = width // DH
    half = heads // 2
    cut = half // 2
    ctx_parts = lax.axis_size("ctx")
    pair = [(0, 1), (1, 0), (2, 3), (3, 2)]
    across = [(0, 2), (2, 0), (1, 3), (3, 1)]
    windows = lax.axis_size("groups")
    first_round, second_round = [], []
    for g in range(windows):
        for c in range(ctx_parts):
            for swaps, there in ((first_round, c ^ 1), (second_round, ((c + 1) ^ 1) - 1)):
                inside = 0 <= there < ctx_parts
                other = g ^ 1 if (g ^ 1) < windows else g
                swaps.append((g * ctx_parts + c, g * ctx_parts + there if inside else other * ctx_parts + c))
    chunk_a, chunk_b = (cut, DH, DH), (half - cut, DH, DH)

    def own_half(a):
        return a % 2 * half * DH

    def other_half(a):
        return (1 - a % 2) * half * DH

    theirs_b, w, masks = opening(lens, at, k, v, lambda a: other_half(a) + cut * DH, half - cut)
    got_b = lax.ppermute(theirs_b, "head", pair)
    theirs_a, own = rest_states(at, masks, k, v, half, cut)
    got_a = lax.ppermute(theirs_a, "head", pair)
    b = small_call(functools.partial(chip_kernel, cut), [w, own, got_b], [chunk_b])
    r1 = lax.ppermute(b, "head", across)
    a = small_call(functools.partial(chip_kernel, 0), [w, own, got_a], [chunk_a])
    r2_odd = lax.ppermute(a, ("groups", "ctx"), first_round)
    r2_even = lax.ppermute(a, ("groups", "ctx"), second_round)
    a, masks = lax.optimization_barrier((a, masks))
    loc0, qm0 = local_part(at, masks, q, k, v, own_half, half)
    r1, loc0 = lax.optimization_barrier((r1, loc0))
    p4 = small_call(carry_kernel, [w, b, r1], [chunk_b])
    r4_odd = lax.ppermute(p4, ("groups", "ctx"), first_round)
    r4_even = lax.ppermute(p4, ("groups", "ctx"), second_round)
    p4, r2_odd, r2_even = lax.optimization_barrier((p4, r2_odd, r2_even))
    p3, r2 = small_call(relay_kernel, [w, a, r2_odd, r2_even], [chunk_a] * 2)
    r3 = lax.ppermute(p3, "head", across)
    p3, masks = lax.optimization_barrier((p3, masks))
    loc1, qm1 = local_part(at, masks, q, k, v, other_half, half)
    r4_odd, loc1 = lax.optimization_barrier((r4_odd, loc1))
    ins = [w, r1, r4_odd, r4_even, own, got_b]
    mine_b, send_b = small_call(functools.partial(join_b_kernel, cut), ins, [chunk_b] * 2)
    other_b = lax.ppermute(send_b, "head", pair)
    r3, mine_b = lax.optimization_barrier((r3, mine_b))
    mine_a, send_a = small_call(join_a_kernel, [w, r3, r2, own, got_a], [chunk_a] * 2)
    other_a = lax.ppermute(send_a, "head", pair)
    chunks = [(loc0, qm0, mine_a, 0), (loc0, qm0, mine_b, cut), (loc1, qm1, other_b, cut), (loc1, qm1, other_a, 0)]
    return finish(at, gain, chunks)


def per_device(queries, keys_in, values, doc_lengths, rms_gain):
    at = jnp.reshape(lax.axis_index(("ctx", "head")).astype(jnp.int32), (1,))
    plan = neighbours if lax.axis_size("head") == 4 else general
    return plan(doc_lengths, at, queries, keys_in, values, rms_gain)


def solution(mesh):
    return jax.shard_map(
        per_device,
        mesh=mesh,
        in_specs=(
            P(("groups", "ctx", "head"), None),
            P(("groups", "ctx", "head"), None),
            P(("groups", "ctx", "head"), None),
            P("groups"),
            P(),
        ),
        out_specs=P(("groups", "ctx", "head"), None),
        check_vma=False,
    )
```
